32 devices in a mesh: row: 8 (over y, x, core), col: 4 (over z).
Axes of the slice: x: 2, y: 2, z: 4, core: 2. Of those that a mesh axis runs over, the one named last changes fastest.
Arguments:
- points: bfloat16 [32768, 256], P(('row', 'col'))
- centres: bfloat16 [2048, 256], replicated, may hold values from -1.5 to 1.5
- picks: int32 [2, 1024], replicated, may hold values from 0 to 32767, as said below
- assign_pts: int32 [32768], P(('row', 'col')), may hold values from 0 to 4095
- cand_assign: int32 [4096, 1], replicated, may hold values from 0 to 1023
Outputs:
- relative_cost: float32 [32768], P(('row', 'col'))
- new_centres: float32 [1024, 256], P('row')
The draws below stay inside these ranges and needn't reach their ends.
Inputs may be any that keep to these rules, and one draw needn't show every extreme that they name: Each row of picks holds 1024 distinct point indices; in each row the points of one device, the block of 1024 consecutive indices, appear at most 64 times, and some device appears exactly 64 times.
All inputs are finite; a program needn't handle non-finite values.
Results may differ from the reference program's by a relative error of at most 0.0005.
Values may be sent and summed in bfloat16 or wider, within the bound.
No kernel may reach another device: no remote copies, remote signals or barrier semaphores. Data moves between devices by JAX's collectives and lax.ppermute only.
A program may use at most 64 MiB of HBM per device.

```python
import math
import jax
import jax.numpy as jnp
import numpy as np
from jax import lax

D = 256
NC0 = 2048
NSAMP = 1024
ROUNDS = 2
K_FINAL = 1024
PTS_DEV = 1024
NPTS = 32768
CAP = 64
K_CAND = 4096


def draw_points(key, part):
    device_total = NPTS // PTS_DEV
    first_key, second_key = jax.random.split(key)
    device_place = (jnp.arange(NPTS) // PTS_DEV).astype(jnp.float32)
    ramp = jnp.exp(math.log(3.0) * device_place / max(device_total - 1, 1))
    row_scale = jnp.exp(jax.random.uniform(second_key, (NPTS, 1), jnp.float32, math.log(0.5), math.log(2.0)))
    base_values = jnp.clip(jax.random.normal(first_key, (NPTS, D), jnp.float32), -6.0, 6.0)
    values = 0.0625 * ramp[:, None] * row_scale * base_values
    return values.astype(jnp.bfloat16)


def draw_picks(key, part):
    device_total = NPTS // PTS_DEV
    slot_total = device_total * CAP
    span_rows = PTS_DEV // CAP

    def one_round(round_key):
        first_key, second_key, third_key, fourth_key = jax.random.split(round_key, 4)
        full_device = jax.random.randint(first_key, (), 0, device_total)
        others = jax.random.permutation(second_key, slot_total - CAP)[:NSAMP - CAP]
        others = jnp.where(others >= full_device * CAP, others + CAP, others)
        slots = jnp.concatenate([full_device * CAP + jnp.arange(CAP), others])
        slots = slots[jax.random.permutation(fourth_key, NSAMP)]
        owner_device = slots // CAP
        within = slots % CAP
        offsets = jax.random.randint(third_key, (NSAMP,), 0, span_rows)
        return (owner_device * PTS_DEV + within * span_rows + offsets).astype(jnp.int32)
    return jax.vmap(one_round)(jax.random.split(key, ROUNDS))


def touch_ends(entries, own_key, low, largest):
    shape = entries.shape
    spot = [jax.random.randint(jax.random.fold_in(own_key, axis), (), 0, shape[axis]) for axis in range(len(shape))]
    entries = entries.at[tuple(spot)].set(low)
    longest = shape.index(max(shape))
    spot[longest] = (spot[longest] + 1) % shape[longest]
    return entries.at[tuple(spot)].set(largest)


def cumulative_ranks(amount, skew):
    loads = [(1 << 20) // math.isqrt(rank ** skew) + 1 for rank in range(1, amount + 1)]
    spread = 1 + sum(loads) // (1 << 30)
    return np.cumsum(np.array([max(1, weight // spread) for weight in loads]))


def ranked_ids(stream_key, shape, count, slope):
    table = cumulative_ranks(count, slope)
    lot = jax.random.randint(jax.random.fold_in(stream_key, 1), shape, 0, int(table[count - 1]))
    standing = jnp.searchsorted(jnp.asarray(table, jnp.int32), lot, side="right")
    return jax.random.permutation(jax.random.fold_in(stream_key, 2), count)[standing].astype(jnp.int32)


def distinct(stream_key, rows, count, top, lift):
    order = jax.random.permutation(jax.random.fold_in(stream_key, 1), count)
    favour = order
    for power in range(3):
        favour = favour * favour // count
    favour = favour * lift // count
    lots = jax.random.randint(jax.random.fold_in(stream_key, 2), (rows, count), 0, 4096) + favour
    holders = jax.random.permutation(jax.random.fold_in(stream_key, 3), rows)[jnp.arange(count) % rows]
    lots = jnp.where(jnp.arange(rows)[:, None] == holders[None, :], 1 << 14, lots)
    priority = lots * count + jnp.arange(count)
    return lax.top_k(priority.astype(jnp.int32), top)[1].astype(jnp.int32)


def bell_draw(own_key, dims, scale, bound, held_as=jnp.bfloat16):
    values = jax.random.normal(own_key, dims, jnp.float32) * scale
    return jnp.minimum(jnp.maximum(values, -bound), bound).astype(held_as)


def setup_inputs(seed: int = 0) -> dict:
    keys = jax.random.split(jax.random.key(seed), 6)
    points = draw_points(jax.random.fold_in(keys[5], 71), 0)
    centres = bell_draw(keys[1], (NC0, D), 0.1, 1.5)
    picks = draw_picks(jax.random.fold_in(keys[5], 71), 0)
    assign_pts = touch_ends(ranked_ids(keys[3], (NPTS,), K_CAND, 2), jax.random.fold_in(keys[3], 3), 0, K_CAND - 1).astype(jnp.int32)
    cand_assign = distinct(keys[4], K_CAND, K_FINAL, 1, 0)
    return dict(points=points, centres=centres, picks=picks, assign_pts=assign_pts, cand_assign=cand_assign)


def reference(points, centres, picks, assign_pts, cand_assign):
    sampled = points[picks.reshape(-1)]
    cand_table = jnp.concatenate([centres, sampled], axis=0)
    table_norms = jnp.sum(jnp.square(cand_table.astype(jnp.float32)), axis=1)

    def block_best(point_block):
        products = jnp.dot(point_block, cand_table.T, preferred_element_type=jnp.float32)
        point_norms = jnp.sum(jnp.square(point_block.astype(jnp.float32)), axis=1)
        distance = point_norms[:, None] + table_norms[None, :] - 2.0 * products
        return jnp.maximum(jnp.min(distance, axis=1), 0.0)

    best = lax.map(block_best, points.reshape(-1, PTS_DEV, D)).reshape(-1)
    total_cost = jnp.sum(best)
    relative_cost = best * NPTS / total_cost
    counts = jax.ops.segment_sum(jnp.ones((NPTS,), jnp.float32), assign_pts, num_segments=K_CAND)
    weights = 1.0 + counts
    weighted = weights[:, None] * cand_table.astype(jnp.float32)
    numerator = jax.ops.segment_sum(weighted, cand_assign[:, 0], num_segments=K_FINAL)
    denominator = jax.ops.segment_sum(weights, cand_assign[:, 0], num_segments=K_FINAL)
    return relative_cost, numerator / denominator[:, None]
```

```python
import functools

import jax
import jax.numpy as jnp
from jax import lax
from jax.experimental import pallas as pl
from jax.experimental.pallas import tpu as pltpu
from jax.sharding import PartitionSpec as P

K_FINAL = 1024
AXES = ("row", "col")
LANES = 128
VMEM_LIMIT = 48 * 1024 * 1024
F32 = jnp.float32
BF16 = jnp.bfloat16

CORE = 4
ORDERS = ((2, 1, 16, 8), (8, 2, 1, 16))


def nt_dot(left, right):
    return lax.dot_general(left, right, (((1,), (1,)), ((), ())), preferred_element_type=F32)


def iota(shape, axis):
    return lax.broadcasted_iota(jnp.int32, shape, axis)


def device_index():
    return lax.axis_index("row") * lax.axis_size("col") + lax.axis_index("col")


def whole_spec():
    return pl.BlockSpec(memory_space=pltpu.VMEM)


def local_call(kernel, out_shape, operands, name, flops=0):
    moved = sum(x.size * x.dtype.itemsize for x in operands)
    return pl.pallas_call(
        kernel,
        out_shape=out_shape,
        in_specs=[whole_spec()] * len(operands),
        out_specs=jax.tree.map(lambda _: whole_spec(), out_shape),
        compiler_params=pltpu.CompilerParams(vmem_limit_bytes=VMEM_LIMIT),
        cost_estimate=pl.CostEstimate(flops=flops, bytes_accessed=moved, transcendentals=0),
        name=name,
    )(*operands)


def pick_kernel(rounds, cap, picks_ref, points_ref, centres_ref, out_ref):
    chunks = picks_ref.shape[0]
    per_round = chunks // rounds
    point_count = points_ref.shape[0]
    slots = out_ref.shape[0]
    local = picks_ref[...] - device_index() * point_count
    owned = (local >= 0) & (local < point_count)
    flags = owned.astype(F32).astype(BF16)
    lower = (iota((LANES, LANES), 0) <= iota((LANES, LANES), 1)).astype(F32).astype(BF16)
    inside = jnp.dot(flags, lower, preferred_element_type=F32)
    sums = jnp.dot(flags, jnp.ones((LANES, LANES), BF16), preferred_element_type=F32)
    first, second = iota((chunks, chunks), 0), iota((chunks, chunks), 1)
    same = lax.div(first, per_round) == lax.div(second, per_round)
    earlier = (same & (second < first)).astype(F32).astype(BF16)
    before = jnp.dot(earlier, sums.astype(BF16), preferred_element_type=F32)
    round_of = lax.div(iota((chunks, LANES), 0), per_round)
    slot = (inside + before).astype(jnp.int32) - 1 + round_of * cap
    slot = jnp.where(owned, slot, -1)
    slot_ids = iota((slots, LANES), 0)
    found = jnp.zeros((slots, LANES), jnp.int32)
    for t in range(chunks):
        found = found + jnp.where(slot[t : t + 1, :] == slot_ids, local[t : t + 1, :] + 1, 0)
    place = jnp.sum(found.astype(F32), axis=1, keepdims=True).astype(jnp.int32)
    chosen = (iota((slots, point_count), 1) + 1 == place).astype(F32).astype(BF16)
    rows = jnp.dot(chosen, points_ref[...], preferred_element_type=F32)
    filler = centres_ref[0:1, :].astype(F32)
    out_ref[...] = jnp.where(place > 0, rows, filler).astype(BF16)


def meta_kernel(rounds, cap, slots, picks_ref, assign_ref, owner_ref, block_ref, count_ref, place_ref, slot_owner_ref):
    chunks = picks_ref.shape[0]
    per_round = chunks // rounds
    cand_chunks = owner_ref.shape[0]
    device_count = block_ref.shape[0]
    slot_chunks = slot_owner_ref.shape[0]
    lane_rows = iota((LANES, LANES), 0)
    tally = jnp.zeros((cand_chunks, LANES), F32)
    for t in range(assign_ref.shape[0]):
        ids = assign_ref[t : t + 1, :]
        high = (lax.div(ids, LANES) == iota((cand_chunks, LANES), 0)).astype(F32).astype(BF16)
        low = (lax.rem(ids, LANES) == lane_rows).astype(F32).astype(BF16)
        tally = tally + nt_dot(high, low)
    count_ref[...] = tally

    lower = (lane_rows <= iota((LANES, LANES), 1)).astype(F32).astype(BF16)
    ones = jnp.ones((LANES, LANES), BF16)
    device_ids = iota((device_count, LANES), 0)
    point_count = assign_ref.shape[0] * LANES
    first_chunk = cand_chunks - chunks
    owners = jnp.zeros((2 * slot_chunks, LANES), F32)
    for r in range(rounds):
        carry = jnp.zeros((device_count, LANES), F32)
        for u in range(per_round):
            t = r * per_round + u
            holder = lax.div(picks_ref[t : t + 1, :], point_count)
            held = (holder == device_ids).astype(F32)
            running = jnp.dot(held.astype(BF16), lower, preferred_element_type=F32) + carry
            carry = carry + jnp.dot(held.astype(BF16), ones, preferred_element_type=F32)
            rank = jnp.sum(held * running, axis=0, keepdims=True).astype(jnp.int32) - 1
            block = jnp.sum(jnp.where(block_ref[...] == holder, device_ids, 0), axis=0, keepdims=True)
            place = block * slots + r * cap + rank
            place_ref[t : t + 1, :] = place
            high = lax.div(place, LANES) == iota((slot_chunks, LANES), 0)
            low = (lax.rem(place, LANES) == lane_rows).astype(F32).astype(BF16)
            tag = owner_ref[first_chunk + t : first_chunk + t + 1, :] + 1
            coarse = jnp.where(high, lax.div(tag, 32).astype(F32), 0.0)
            fine = jnp.where(high, lax.rem(tag, 32).astype(F32), 0.0)
            owners = owners + nt_dot(jnp.concatenate([coarse, fine], axis=0).astype(BF16), low)
    slot_owner_ref[...] = (owners[:slot_chunks] * 32.0 + owners[slot_chunks:]).astype(jnp.int32) - 1


def scan_pieces(points_ref, piece_refs, best):
    points = points_ref[...]
    for piece_ref in piece_refs:
        rows = piece_ref.shape[0]
        step = min(256, rows)

        def visit(i, best, piece_ref=piece_ref, step=step):
            piece = piece_ref[pl.ds(pl.multiple_of(i * step, step), step), :]
            wide = piece.astype(F32)
            half = 0.5 * jnp.sum(wide * wide, axis=1, keepdims=True)
            score = nt_dot(piece, points) - half
            for k in range(step // 8):
                best = jnp.maximum(best, score[k * 8 : k * 8 + 8, :])
            return best

        best = lax.fori_loop(0, rows // step, visit, best)
    return best


def first_scan_kernel(points_ref, *refs):
    best = jnp.full((8, points_ref.shape[0]), -jnp.inf, F32)
    refs[-1][...] = scan_pieces(points_ref, refs[:-1], best)


def next_scan_kernel(points_ref, best_ref, *refs):
    refs[-1][...] = scan_pieces(points_ref, refs[:-1], best_ref[...])


def last_scan_kernel(points_ref, best_ref, *refs):
    near_ref, share_ref = refs[-2:]
    best = scan_pieces(points_ref, refs[:-2], best_ref[...])
    best = jnp.max(best, axis=0, keepdims=True)
    wide = points_ref[...].astype(F32)
    square = wide * wide
    top = square.astype(BF16)
    rest = (square - top.astype(F32)).astype(BF16)
    ones = jnp.ones((8, square.shape[1]), BF16)
    norm = (nt_dot(ones, top) + nt_dot(ones, rest))[0:1, :]
    near = jnp.maximum(norm - 2.0 * best, 0.0)
    near_ref[...] = near
    share_ref[...] = jnp.broadcast_to(jnp.sum(near, axis=1, keepdims=True)[None], share_ref.shape)


def scale_kernel(total_points, near_ref, share_ref, out_ref):
    total = jnp.sum(share_ref[...], axis=0)[0:1, 0:1]
    out_ref[...] = near_ref[...] * total_points / total


def lloyd_kernel(count_ref, owner_ref, place_ref, slot_owner_ref, centres_ref, *refs):
    piece_refs, out_ref = refs[:-1], refs[-1]
    finals = out_ref.shape[0]
    slot_chunks = slot_owner_ref.shape[0]
    chunks = place_ref.shape[0]
    first_chunks = owner_ref.shape[0] - chunks
    weights = 1.0 + count_ref[...]
    weight_top = weights.astype(BF16).astype(F32)
    weight_rest = (weights - weight_top).astype(BF16).astype(F32)
    lane_rows = iota((LANES, LANES), 0)
    placed = jnp.zeros((2 * slot_chunks, LANES), F32)
    for t in range(chunks):
        place = place_ref[t : t + 1, :]
        high = lax.div(place, LANES) == iota((slot_chunks, LANES), 0)
        low = (lax.rem(place, LANES) == lane_rows).astype(F32).astype(BF16)
        c = first_chunks + t
        both = [jnp.where(high, w[c : c + 1, :], 0.0) for w in (weight_top, weight_rest)]
        placed = placed + nt_dot(jnp.concatenate(both, axis=0).astype(BF16), low)
    targets = iota((finals, LANES), 0) + lax.axis_index("row") * finals

    def add_rows(carried, rows_ref, owners, tops, rests):
        total, mass = carried
        parts = []
        for b in range(owners.shape[0]):
            mine = owners[b : b + 1, :] == targets
            top = jnp.where(mine, tops[b : b + 1, :], 0.0)
            rest = jnp.where(mine, rests[b : b + 1, :], 0.0)
            mass = mass + (top + rest)
            parts.append(jnp.concatenate([top, rest], axis=0).astype(BF16))
        member = jnp.concatenate(parts, axis=1)
        return total + jnp.dot(member, rows_ref[...], preferred_element_type=F32), mass

    carried = (jnp.zeros((2 * finals, centres_ref.shape[1]), F32), jnp.zeros((finals, LANES), F32))
    carried = add_rows(
        carried, centres_ref, owner_ref[:first_chunks, :], weight_top[:first_chunks], weight_rest[:first_chunks]
    )
    start = 0
    for piece_ref in piece_refs:
        stop = start + piece_ref.shape[0] // LANES
        carried = add_rows(
            carried,
            piece_ref,
            slot_owner_ref[start:stop, :],
            placed[start:stop],
            placed[slot_chunks + start : slot_chunks + stop],
        )
        start = stop
    total, mass = carried
    out_ref[...] = (total[:finals] + total[finals:]) / jnp.sum(mass, axis=1, keepdims=True)


def xor_pairs(masks):
    return [(d, d ^ masks[(d // CORE) % 2]) for d in range(32)]


def block_order(doubling):
    device_count = lax.axis_size("row") * lax.axis_size("col")
    ids = jnp.arange(device_count, dtype=jnp.int32)
    if not doubling:
        return ids
    me = device_index()
    tables = []
    for mine in (0, 1):
        table = []
        for other in (0, 1):
            for q in range(16):
                mask = CORE * other
                for k in range(4):
                    if (q >> k) & 1:
                        mask ^= ORDERS[mine ^ other][k]
                table.append(mask)
        tables.append([table[i] for i in range(32)])
    core = lax.rem(lax.div(me, CORE), 2)
    return jnp.where(core == 0, jnp.array(tables[0], jnp.int32), jnp.array(tables[1], jnp.int32)) ^ me


def shards(points, centres, picks, assign_pts, cand_assign):
    point_count, feature_count = points.shape
    row_count, col_count = lax.axis_size("row"), lax.axis_size("col")
    device_count = row_count * col_count
    doubling = (row_count, col_count) == (8, 4)
    round_count, sample_count = picks.shape
    cand_count = centres.shape[0] + round_count * sample_count
    cap = min(point_count, sample_count, -(-2 * sample_count // device_count))
    slots = -(-round_count * cap // 16) * 16
    slot_chunks = device_count * slots // LANES
    pick_rows = picks.reshape(-1, LANES)
    chunks = pick_rows.shape[0]
    shape = jax.ShapeDtypeStruct

    block = local_call(
        functools.partial(pick_kernel, round_count, cap),
        shape((slots, feature_count), BF16),
        (pick_rows, points, centres[:16]),
        "pick_rows",
    )
    order = jnp.broadcast_to(block_order(doubling)[:, None], (device_count, LANES))
    owner_rows = cand_assign.reshape(-1, LANES)
    counts, places, slot_owners = local_call(
        functools.partial(meta_kernel, round_count, cap, slots),
        (
            shape((cand_count // LANES, LANES), F32),
            shape((chunks, LANES), jnp.int32),
            shape((slot_chunks, LANES), jnp.int32),
        ),
        (pick_rows, assign_pts.reshape(-1, LANES), owner_rows, order),
        "slot_owners",
    )
    best_shape = shape((8, point_count), F32)
    scan_flops = 2 * point_count * feature_count

    def first_scan(pieces):
        rows = sum(p.shape[0] for p in pieces)
        return local_call(first_scan_kernel, best_shape, (points, *pieces), "scan_centres", scan_flops * rows)

    def next_scan(best, pieces):
        rows = sum(p.shape[0] for p in pieces)
        return local_call(next_scan_kernel, best_shape, (points, best, *pieces), "scan_sampled", scan_flops * rows)

    def last_scan(best, pieces):
        rows = sum(p.shape[0] for p in pieces)
        return local_call(
            last_scan_kernel,
            (shape((1, point_count), F32), shape((device_count, 8, LANES), F32)),
            (points, best, *pieces),
            "scan_last",
            scan_flops * rows,
        )

    best = first_scan([centres])
    if doubling:
        buffer = block
        for k in range(4):
            pairs = xor_pairs((ORDERS[0][k], ORDERS[1][k]))
            received = lax.ppermute(buffer, AXES, pairs)
            counts = counts + lax.ppermute(counts, AXES, pairs)
            if k < 3:
                buffer = jnp.concatenate([buffer, received], axis=0)
        swap = xor_pairs((CORE, CORE))
        counts = counts + lax.ppermute(counts, AXES, swap)
        early = lax.ppermute(buffer, AXES, swap)
        late = lax.ppermute(received, AXES, swap)
        pieces = [buffer, received, early, late]
        best = next_scan(best, [buffer, early])
        best = next_scan(best, [received])
        near, share = last_scan(best, [late])
        shares = lax.all_to_all(share, AXES, 0, 0)
    else:
        counts = lax.psum(counts, AXES)
        pieces = [lax.all_gather(block, AXES, tiled=True)]
        near, share = last_scan(best, pieces)
        shares = lax.psum(share[:1], AXES)
    relative = local_call(
        functools.partial(scale_kernel, float(point_count * device_count)),
        shape((1, point_count), F32),
        (near, shares),
        "relative",
    )
    new_centres = local_call(
        lloyd_kernel,
        shape((K_FINAL // row_count, feature_count), F32),
        (counts, owner_rows, places, slot_owners, centres, *pieces),
        "lloyd",
        4 * K_FINAL // row_count * feature_count * cand_count,
    )
    return (relative.reshape(-1), new_centres)


def solution(mesh):
    placed = (P(AXES, None), P(), P(), P(AXES), P())
    return jax.shard_map(
        shards,
        mesh=mesh,
        in_specs=placed,
        out_specs=(P(AXES), P("row", None)),
        check_vma=False,
    )
```

```python
import functools

import jax
import jax.numpy as jnp
from jax import lax
from jax.experimental import pallas as pl
from jax.experimental.pallas import tpu as pltpu
from jax.sharding import PartitionSpec as P

K_FINAL = 1024
AXES = ("row", "col")
LANES = 128
VMEM_LIMIT = 20 * 1024 * 1024
FLOPS_PER_US = 1.0e9
F32 = jnp.float32
BF16 = jnp.bfloat16

CORE = 4
FAN = ((1, 2), (8, 1))
SPREAD = ((8, 16), (16, 2))


def nt_dot(left, right):
    return lax.dot_general(left, right, (((1,), (1,)), ((), ())), preferred_element_type=F32)


def iota(shape, axis):
    return lax.broadcasted_iota(jnp.int32, shape, axis)


def device_index():
    return lax.axis_index("row") * lax.axis_size("col") + lax.axis_index("col")


def whole_spec():
    return pl.BlockSpec(memory_space=pltpu.VMEM)


def local_call(kernel, out_shape, operands, name, cost, after=(), unread=(), scratch=(), vmem=VMEM_LIMIT):
    specs = [whole_spec()] * len(operands) + [pl.BlockSpec(memory_space=pl.ANY)] * len(after)
    operands = list(operands)
    for place in unread:
        specs[place] = pl.BlockSpec(memory_space=pltpu.HBM)
        operands[place] = pltpu.with_memory_space_constraint(operands[place], pltpu.HBM)
    count = len(operands)

    def body(*refs):
        kernel(*refs[:count], *refs[count + len(after) :])

    return pl.pallas_call(
        body,
        out_shape=out_shape,
        in_specs=specs,
        out_specs=jax.tree.map(lambda _: whole_spec(), out_shape),
        scratch_shapes=list(scratch),
        compiler_params=pltpu.CompilerParams(vmem_limit_bytes=vmem),
        cost_estimate=pl.CostEstimate(flops=int(cost * FLOPS_PER_US), bytes_accessed=0, transcendentals=0),
        name=name,
    )(*operands, *after)


def chunk_rows(ref):
    rounds, samples = ref.shape
    return jnp.concatenate(
        [ref[r : r + 1, k : k + LANES] for r in range(rounds) for k in range(0, samples, LANES)], axis=0
    )


FAR = 2.0**64


def pick_kernel(cap, slots, picks_hbm, points_hbm, assign_hbm, out_ref, picks_ref, points_ref, assign_ref, sems):
    picks_copy = pltpu.make_async_copy(picks_hbm, picks_ref, sems.at[0])
    assign_copy = pltpu.make_async_copy(assign_hbm, assign_ref, sems.at[1])
    points_copy = pltpu.make_async_copy(points_hbm, points_ref, sems.at[2])
    picks_copy.start()
    assign_copy.start()
    points_copy.start()
    picks_copy.wait()
    rounds = picks_ref.shape[0]
    per_round = picks_ref.shape[1] // LANES
    chunks = rounds * per_round
    point_count = points_ref.shape[0]
    local = chunk_rows(picks_ref) - device_index() * point_count
    owned = (local >= 0) & (local < point_count)
    flags = owned.astype(F32).astype(BF16)
    lower = (iota((LANES, LANES), 0) <= iota((LANES, LANES), 1)).astype(F32).astype(BF16)
    inside = jnp.dot(flags, lower, preferred_element_type=F32)
    sums = jnp.dot(flags, jnp.ones((LANES, LANES), BF16), preferred_element_type=F32)
    first, second = iota((chunks, chunks), 0), iota((chunks, chunks), 1)
    same = lax.div(first, per_round) == lax.div(second, per_round)
    earlier = (same & (second < first)).astype(F32).astype(BF16)
    before = jnp.dot(earlier, sums.astype(BF16), preferred_element_type=F32)
    round_of = lax.div(iota((chunks, LANES), 0), per_round)
    slot = (inside + before).astype(jnp.int32) - 1 + round_of * cap
    slot = jnp.where(owned, slot, -1)
    slot_ids = iota((slots, LANES), 0)
    found = jnp.zeros((slots, LANES), jnp.int32)
    for t in range(chunks):
        found = found + jnp.where(slot[t : t + 1, :] == slot_ids, local[t : t + 1, :] + 1, 0)
    place = jnp.sum(found.astype(F32), axis=1, keepdims=True).astype(jnp.int32)
    chosen = (iota((slots, point_count), 1) + 1 == place).astype(F32).astype(BF16)
    assign_copy.wait()
    ids = assign_ref[...]
    ids = jnp.concatenate([lax.div(ids, LANES), lax.rem(ids, LANES)], axis=1).astype(F32)
    spare = jnp.zeros((out_ref.shape[0] - slots - ids.shape[0], ids.shape[1]), F32)
    points_copy.wait()
    rows = jnp.dot(chosen, points_ref[...], preferred_element_type=F32)
    rows = jnp.where(place > 0, rows, FAR)
    out_ref[...] = jnp.concatenate([rows, ids, spare], axis=0).astype(BF16)


def add_tally(count, piece_ref, slots, id_rows):
    block_rows = slots + -(-id_rows // 16) * 16
    cand_chunks = count.shape[0]
    lane_rows = iota((LANES, LANES), 0).astype(F32)
    chunk_ids = iota((cand_chunks, LANES), 0).astype(F32)
    for start in range(slots, piece_ref.shape[0], block_rows):
        ids = piece_ref[start : start + block_rows - slots, :].astype(F32)
        high = [(ids[t : t + 1, :LANES] == chunk_ids).astype(F32) for t in range(id_rows)]
        low = [(ids[t : t + 1, LANES:] == lane_rows).astype(F32) for t in range(id_rows)]
        high = jnp.concatenate(high, axis=1).astype(BF16)
        low = jnp.concatenate(low, axis=1).astype(BF16)
        count = count + nt_dot(high, low)
    return count


def tally_kernel(slots, id_rows, piece_ref, count_ref):
    count_ref[...] = add_tally(jnp.zeros(count_ref.shape, F32), piece_ref, slots, id_rows)


def holders_in_order(doubling, device_ids):
    if not doubling:
        return device_ids
    me = device_index()
    core = lax.rem(lax.div(me, CORE), 2)
    other = lax.div(device_ids, 16)
    kind = core ^ other
    mask = other * CORE
    for bit, masks in enumerate((*zip(*FAN), *zip(*SPREAD))):
        present = lax.rem(lax.div(device_ids, 1 << bit), 2)
        mask = mask ^ (present * jnp.where(kind == 0, masks[0], masks[1]))
    return me ^ mask


def slot_kernel(doubling, cap, slots, device_count, point_count, picks_ref, owner_ref, start_ref, place_ref, slot_owner_ref, token_ref):
    token_ref[...] = start_ref[...]
    picks = chunk_rows(picks_ref)
    chunks = picks.shape[0]
    rounds = picks_ref.shape[0]
    per_round = chunks // rounds
    cand_chunks = owner_ref.shape[0]
    slot_chunks = slot_owner_ref.shape[0]
    lane_rows = iota((LANES, LANES), 0)
    lower = (lane_rows <= iota((LANES, LANES), 1)).astype(F32).astype(BF16)
    ones = jnp.ones((LANES, LANES), BF16)
    device_ids = iota((device_count, LANES), 0)
    first_chunk = cand_chunks - chunks
    holders = holders_in_order(doubling, device_ids)
    owners = jnp.zeros((2 * slot_chunks, LANES), F32)
    for r in range(rounds):
        carry = jnp.zeros((device_count, LANES), F32)
        for u in range(per_round):
            t = r * per_round + u
            holder = lax.div(picks[t : t + 1, :], point_count)
            held = (holder == device_ids).astype(F32)
            running = jnp.dot(held.astype(BF16), lower, preferred_element_type=F32) + carry
            carry = carry + jnp.dot(held.astype(BF16), ones, preferred_element_type=F32)
            rank = jnp.sum(held * running, axis=0, keepdims=True).astype(jnp.int32) - 1
            block = jnp.sum(jnp.where(holders == holder, device_ids, 0), axis=0, keepdims=True)
            place = block * slots + r * cap + rank
            place_ref[t : t + 1, :] = place
            high = lax.div(place, LANES) == iota((slot_chunks, LANES), 0)
            low = (lax.rem(place, LANES) == lane_rows).astype(F32).astype(BF16)
            tag = owner_ref[first_chunk + t : first_chunk + t + 1, :] + 1
            coarse = jnp.where(high, lax.div(tag, 32).astype(F32), 0.0)
            fine = jnp.where(high, lax.rem(tag, 32).astype(F32), 0.0)
            owners = owners + nt_dot(jnp.concatenate([coarse, fine], axis=0).astype(BF16), low)
    slot_owner_ref[...] = (owners[:slot_chunks] * 32.0 + owners[slot_chunks:]).astype(jnp.int32) - 1


def scan_rows(points, piece, best):
    wide = piece.astype(F32)
    half = 0.5 * jnp.sum(wide * wide, axis=1, keepdims=True)
    score = nt_dot(piece, points) - half
    for k in range(0, piece.shape[0], 8):
        best = jnp.maximum(best, score[k : k + 8, :])
    return best


def slot_rows(piece_ref, slots, block_rows):
    return [piece_ref[k : k + slots, :] for k in range(0, piece_ref.shape[0], block_rows)]


def scan_table(points_ref, table_ref, best):
    points = points_ref[...]
    rows = table_ref.shape[0]
    step = min(256, rows)
    if rows <= 4096:
        for start in range(0, rows, step):
            best = scan_rows(points, table_ref[start : start + step, :], best)
        return best

    def visit(i, best):
        return scan_rows(points, table_ref[pl.ds(pl.multiple_of(i * step, step), step), :], best)

    return lax.fori_loop(0, rows // step, visit, best)


def scan_pieces(points_ref, piece_refs, best, slots, block_rows):
    points = points_ref[...]
    for piece_ref in piece_refs:
        blocks = slot_rows(piece_ref, slots, block_rows)
        for k in range(0, len(blocks), 2):
            best = scan_rows(points, jnp.concatenate(blocks[k : k + 2], axis=0), best)
    return best


def first_scan_kernel(points_ref, centres_ref, best_ref, norm_ref, token_ref):
    token_ref[...] = jnp.zeros(token_ref.shape, F32)
    best_ref[...] = scan_table(points_ref, centres_ref, jnp.full(best_ref.shape, -jnp.inf, F32))
    wide = points_ref[...].astype(F32)
    square = wide * wide
    top = square.astype(BF16)
    rest = (square - top.astype(F32)).astype(BF16)
    ones = jnp.ones((8, square.shape[1]), BF16)
    norm_ref[...] = nt_dot(ones, top) + nt_dot(ones, rest)


def next_scan_kernel(slots, block_rows, id_rows, points_ref, best_ref, count_ref, *refs):
    next_ref, next_count_ref, token_ref = refs[-3:]
    token_ref[...] = jnp.zeros(token_ref.shape, F32)
    next_ref[...] = scan_pieces(points_ref, refs[:-3], best_ref[...], slots, block_rows)
    count = count_ref[...]
    if id_rows:
        for piece_ref in refs[:-3]:
            count = add_tally(count, piece_ref, slots, id_rows)
    next_count_ref[...] = count


def last_scan_kernel(slots, block_rows, points_ref, best_ref, norm_ref, piece_ref, near_ref, share_ref):
    if block_rows:
        best = scan_pieces(points_ref, [piece_ref], best_ref[...], slots, block_rows)
    else:
        best = scan_table(points_ref, piece_ref, best_ref[...])
    near = jnp.maximum(norm_ref[0:1, :] - 2.0 * jnp.max(best, axis=0, keepdims=True), 0.0)
    near_ref[...] = near
    share_ref[...] = jnp.broadcast_to(jnp.sum(near, axis=1, keepdims=True)[None], share_ref.shape)


def lloyd_kernel(slots, block_rows, id_rows, count_ref, owner_ref, place_ref, slot_owner_ref, centres_ref, *refs):
    piece_refs, out_ref = refs[:-1], refs[-1]
    finals = out_ref.shape[0]
    slot_chunks = slot_owner_ref.shape[0]
    chunks = place_ref.shape[0]
    first_chunks = owner_ref.shape[0] - chunks
    count = count_ref[...]
    for k in id_rows:
        count = add_tally(count, piece_refs[k], slots, id_rows[k])
    weights = 1.0 + count
    weight_top = weights.astype(BF16).astype(F32)
    weight_rest = (weights - weight_top).astype(BF16).astype(F32)
    lane_rows = iota((LANES, LANES), 0)
    placed = jnp.zeros((2 * slot_chunks, LANES), F32)
    for t in range(chunks):
        place = place_ref[t : t + 1, :]
        high = lax.div(place, LANES) == iota((slot_chunks, LANES), 0)
        low = (lax.rem(place, LANES) == lane_rows).astype(F32).astype(BF16)
        c = first_chunks + t
        both = [jnp.where(high, w[c : c + 1, :], 0.0) for w in (weight_top, weight_rest)]
        placed = placed + nt_dot(jnp.concatenate(both, axis=0).astype(BF16), low)
    targets = iota((finals, LANES), 0) + lax.axis_index("row") * finals

    def members(owners, tops, rests, mass):
        parts = []
        for b in range(owners.shape[0]):
            mine = owners[b : b + 1, :] == targets
            top = jnp.where(mine, tops[b : b + 1, :], 0.0)
            rest = jnp.where(mine, rests[b : b + 1, :], 0.0)
            mass = mass + (top + rest)
            parts.append(jnp.concatenate([top, rest], axis=0).astype(BF16))
        return jnp.concatenate(parts, axis=1), mass

    mass = jnp.zeros((finals, LANES), F32)
    member, mass = members(owner_ref[:first_chunks, :], weight_top[:first_chunks], weight_rest[:first_chunks], mass)
    total = jnp.dot(member, centres_ref[...], preferred_element_type=F32)
    start = 0
    for piece_ref in piece_refs:
        rows = jnp.concatenate(slot_rows(piece_ref, slots, block_rows), axis=0) if block_rows else piece_ref[...]
        stop = start + rows.shape[0] // LANES
        member, mass = members(
            slot_owner_ref[start:stop, :], placed[start:stop], placed[slot_chunks + start : slot_chunks + stop], mass
        )
        total = total + jnp.dot(member, rows, preferred_element_type=F32)
        start = stop
    out_ref[...] = (total[:finals] + total[finals:]) / jnp.sum(mass, axis=1, keepdims=True)


def finish_kernel(total_points, near_ref, share_ref, relative_ref):
    cost = jnp.sum(share_ref[...], axis=0)[0:1, 0:1]
    relative_ref[...] = near_ref[...] * total_points / cost


def permute(value, masks):
    pairs = [(d, d ^ masks[(d // CORE) % 2]) for d in range(lax.axis_size(AXES))]
    return lax.ppermute(value, AXES, pairs)


def hop(index):
    masks = tuple(zip(*FAN)) + tuple(zip(*SPREAD))
    return masks[index]


def done_after(value, *tokens):
    ready = tokens[0] >= 0.0
    for token in tokens[1:]:
        ready = ready & (token >= 0.0)
    return jnp.where(ready[:, : value.shape[1]], value, jnp.zeros_like(value))


def both_hops(first, second):
    return tuple(a ^ b for a, b in zip(first, second))


def shards(points, centres, picks, assign_pts, cand_assign):
    point_count, feature_count = points.shape
    row_count, col_count = lax.axis_size("row"), lax.axis_size("col")
    device_count = row_count * col_count
    doubling = (row_count, col_count) == (8, 4)
    round_count, sample_count = picks.shape
    cand_count = centres.shape[0] + round_count * sample_count
    cap = min(point_count, sample_count, -(-2 * sample_count // device_count))
    slots = -(-round_count * cap // 16) * 16
    slot_chunks = device_count * slots // LANES
    chunks = round_count * sample_count // LANES
    finals = K_FINAL // row_count
    shape = jax.ShapeDtypeStruct

    token = shape((1, feature_count), F32)
    id_rows = point_count // LANES
    block_rows = slots + -(-id_rows // 16) * 16
    block = local_call(
        functools.partial(pick_kernel, cap, slots),
        shape((block_rows, feature_count), BF16),
        (picks, points, assign_pts.reshape(id_rows, LANES)),
        "pick_rows",
        0.8,
        unread=(0, 1, 2),
        scratch=(
            pltpu.VMEM(picks.shape, jnp.int32),
            pltpu.VMEM(points.shape, BF16),
            pltpu.VMEM((id_rows, LANES), jnp.int32),
            pltpu.SemaphoreType.DMA((3,)),
        ),
    )
    count_shape = shape((cand_count // LANES, LANES), F32)
    owner_rows = cand_assign.reshape(-1, LANES)

    def find_slots(start):
        results = (shape((chunks, LANES), jnp.int32), shape((slot_chunks, LANES), jnp.int32), token)
        kernel = functools.partial(slot_kernel, doubling, cap, slots, device_count, point_count)
        return local_call(kernel, results, (picks, owner_rows, start), "slot_owners", 1.0)

    best_shape = shape((8, point_count), F32)

    best, norms, scanned = local_call(
        first_scan_kernel, (best_shape, best_shape, token), (points, centres), "scan_centres", 1.6
    )

    def next_scan(best, counts, tallied, *pieces):
        cost = 0.1 + 0.8e-3 * sum(p.shape[0] for p in pieces)
        kernel = functools.partial(next_scan_kernel, slots, block_rows, id_rows if tallied else 0)
        results = (best_shape, count_shape, token)
        return local_call(kernel, results, (points, best, counts, *pieces), "scan_sampled", cost)

    def last_scan(best, piece, split):
        cost = 0.5 + 0.8e-3 * piece.shape[0]
        kernel = functools.partial(last_scan_kernel, slots, block_rows if split else 0)
        results = (shape((1, point_count), F32), shape((device_count, 1, LANES), F32))
        return local_call(kernel, results, (points, best, norms, piece), "scan_last", cost)

    if doubling:
        swap = (CORE, CORE)
        near = [block, *(permute(block, m) for m in (hop(0), hop(1), both_hops(hop(0), hop(1))))]
        own = done_after(jnp.concatenate(near, axis=0), scanned)
        first = permute(own, hop(2))
        second = permute(own, hop(3))
        swapped = [permute(own, swap)]
        places, slot_owners, found = find_slots(scanned)
        counts = jnp.zeros(count_shape.shape, F32)
        best, counts, scanned = next_scan(best, counts, True, own, swapped[0])
        third = permute(done_after(first, scanned, found), hop(3))
        swapped += [permute(first, swap), permute(second, swap)]
        best, counts, scanned = next_scan(best, counts, True, first, second, swapped[1], swapped[2])
        swapped.append(permute(done_after(third, scanned), swap))
        best, counts, scanned = next_scan(best, counts, False, third)
        near, share = last_scan(best, swapped[3], True)
        shares = lax.all_to_all(share, AXES, 0, 0)
        pieces = (own, first, second, third, *swapped)
        untold = {3: id_rows, 7: id_rows}
    else:
        places, slot_owners, found = find_slots(scanned)
        counts = local_call(
            functools.partial(tally_kernel, slots, id_rows), count_shape, (block,), "tally", 0.3
        )
        counts = lax.psum(counts, AXES)
        pieces = (lax.all_gather(block[:slots], AXES, tiled=True),)
        near, share = last_scan(best, pieces[0], False)
        shares = lax.psum(share[:1], AXES)
        untold = {}
    new_centres = local_call(
        functools.partial(lloyd_kernel, slots, block_rows if doubling else 0, untold),
        shape((finals, feature_count), F32),
        (counts, owner_rows, places, slot_owners, centres, *pieces),
        "lloyd",
        2.6,
    )
    relative = local_call(
        functools.partial(finish_kernel, float(point_count * device_count)),
        shape((1, point_count), F32),
        (near, shares),
        "finish",
        0.6,
    )
    return (relative.reshape(-1), new_centres)


def solution(mesh):
    placed = (P(AXES, None), P(), P(), P(AXES), P())
    return jax.shard_map(
        shards,
        mesh=mesh,
        in_specs=placed,
        out_specs=(P(AXES), P("row", None)),
        check_vma=False,
    )
```

```python
import functools

import jax
import jax.numpy as jnp
from jax import lax
from jax.experimental import pallas as pl
from jax.experimental.pallas import tpu as pltpu
from jax.sharding import PartitionSpec as P

K_FINAL = 1024
AXES = ("row", "col")
LANES = 128
VMEM_LIMIT = 20 * 1024 * 1024
FLOPS_PER_US = 1.0e9
F32 = jnp.float32
BF16 = jnp.bfloat16

CORE = 4
FAN = ((1, 2), (8, 1))
SPREAD = ((16, 8), (2, 16))


def nt_dot(left, right):
    return lax.dot_general(left, right, (((1,), (1,)), ((), ())), preferred_element_type=F32)


def iota(shape, axis):
    return lax.broadcasted_iota(jnp.int32, shape, axis)


def device_index():
    return lax.axis_index("row") * lax.axis_size("col") + lax.axis_index("col")


def whole_spec():
    return pl.BlockSpec(memory_space=pltpu.VMEM)


def local_call(kernel, out_shape, operands, name, cost, after=(), unread=(), scratch=(), vmem=VMEM_LIMIT):
    specs = [whole_spec()] * len(operands) + [pl.BlockSpec(memory_space=pl.ANY)] * len(after)
    operands = list(operands)
    for place in unread:
        specs[place] = pl.BlockSpec(memory_space=pltpu.HBM)
        operands[place] = pltpu.with_memory_space_constraint(operands[place], pltpu.HBM)
    count = len(operands)

    def body(*refs):
        kernel(*refs[:count], *refs[count + len(after) :])

    return pl.pallas_call(
        body,
        out_shape=out_shape,
        in_specs=specs,
        out_specs=jax.tree.map(lambda _: whole_spec(), out_shape),
        scratch_shapes=list(scratch),
        compiler_params=pltpu.CompilerParams(vmem_limit_bytes=vmem),
        cost_estimate=pl.CostEstimate(flops=int(cost * FLOPS_PER_US), bytes_accessed=0, transcendentals=0),
        name=name,
    )(*operands, *after)


def chunk_rows(ref):
    rounds, samples = ref.shape
    return jnp.concatenate(
        [ref[r : r + 1, k : k + LANES] for r in range(rounds) for k in range(0, samples, LANES)], axis=0
    )


FAR = 2.0**64


def pick_kernel(cap, slots, picks_hbm, points_hbm, assign_hbm, out_ref, picks_ref, points_ref, assign_ref, sems):
    picks_copy = pltpu.make_async_copy(picks_hbm, picks_ref, sems.at[0])
    assign_copy = pltpu.make_async_copy(assign_hbm, assign_ref, sems.at[1])
    points_copy = pltpu.make_async_copy(points_hbm, points_ref, sems.at[2])
    picks_copy.start()
    assign_copy.start()
    points_copy.start()
    picks_copy.wait()
    rounds = picks_ref.shape[0]
    per_round = picks_ref.shape[1] // LANES
    chunks = rounds * per_round
    point_count = points_ref.shape[0]
    local = chunk_rows(picks_ref) - device_index() * point_count
    owned = (local >= 0) & (local < point_count)
    flags = owned.astype(F32).astype(BF16)
    lower = (iota((LANES, LANES), 0) <= iota((LANES, LANES), 1)).astype(F32).astype(BF16)
    inside = jnp.dot(flags, lower, preferred_element_type=F32)
    sums = jnp.dot(flags, jnp.ones((LANES, LANES), BF16), preferred_element_type=F32)
    first, second = iota((chunks, chunks), 0), iota((chunks, chunks), 1)
    same = lax.div(first, per_round) == lax.div(second, per_round)
    earlier = (same & (second < first)).astype(F32).astype(BF16)
    before = jnp.dot(earlier, sums.astype(BF16), preferred_element_type=F32)
    round_of = lax.div(iota((chunks, LANES), 0), per_round)
    slot = (inside + before).astype(jnp.int32) - 1 + round_of * cap
    slot = jnp.where(owned, slot, -1)
    slot_ids = iota((slots, LANES), 0)
    found = jnp.zeros((slots, LANES), jnp.int32)
    for t in range(chunks):
        found = found + jnp.where(slot[t : t + 1, :] == slot_ids, local[t : t + 1, :] + 1, 0)
    place = jnp.sum(found.astype(F32), axis=1, keepdims=True).astype(jnp.int32)
    chosen = (iota((slots, point_count), 1) + 1 == place).astype(F32).astype(BF16)
    assign_copy.wait()
    ids = assign_ref[...]
    ids = jnp.concatenate([lax.div(ids, LANES), lax.rem(ids, LANES)], axis=1).astype(F32)
    spare = jnp.zeros((out_ref.shape[0] - slots - ids.shape[0], ids.shape[1]), F32)
    points_copy.wait()
    rows = jnp.dot(chosen, points_ref[...], preferred_element_type=F32)
    rows = jnp.where(place > 0, rows, FAR)
    out_ref[...] = jnp.concatenate([rows, ids, spare], axis=0).astype(BF16)


def add_tally(count, ids):
    cand_chunks = count.shape[0]
    lane_rows = iota((LANES, LANES), 0).astype(F32)
    chunk_ids = iota((cand_chunks, LANES), 0).astype(F32)
    ids = ids.astype(F32)
    for start in range(0, ids.shape[0], 8):
        rows = [ids[t : t + 1, :] for t in range(start, start + 8)]
        high = [(row[:, :LANES] == chunk_ids).astype(F32) for row in rows]
        low = [(row[:, LANES:] == lane_rows).astype(F32) for row in rows]
        high = jnp.concatenate(high, axis=1).astype(BF16)
        low = jnp.concatenate(low, axis=1).astype(BF16)
        count = count + nt_dot(high, low)
    return count


def tally_kernel(ids_ref, count_ref):
    count_ref[...] = add_tally(jnp.zeros(count_ref.shape, F32), ids_ref[...])


def holders_in_order(doubling, device_ids):
    if not doubling:
        return device_ids
    me = device_index()
    core = lax.rem(lax.div(me, CORE), 2)
    other = lax.div(device_ids, 16)
    kind = core ^ other
    mask = other * CORE
    for bit, masks in enumerate((*zip(*FAN), *zip(*SPREAD))):
        present = lax.rem(lax.div(device_ids, 1 << bit), 2)
        mask = mask ^ (present * jnp.where(kind == 0, masks[0], masks[1]))
    return me ^ mask


def slot_kernel(doubling, cap, slots, device_count, point_count, picks_ref, owner_ref, place_ref, slot_owner_ref, token_ref):
    token_ref[...] = jnp.zeros(token_ref.shape, F32)
    picks = chunk_rows(picks_ref)
    chunks = picks.shape[0]
    rounds = picks_ref.shape[0]
    per_round = chunks // rounds
    cand_chunks = owner_ref.shape[0]
    slot_chunks = slot_owner_ref.shape[0]
    lane_rows = iota((LANES, LANES), 0)
    lower = (lane_rows <= iota((LANES, LANES), 1)).astype(F32).astype(BF16)
    ones = jnp.ones((LANES, LANES), BF16)
    device_ids = iota((device_count, LANES), 0)
    first_chunk = cand_chunks - chunks
    holders = holders_in_order(doubling, device_ids)
    owners = jnp.zeros((2 * slot_chunks, LANES), F32)
    for r in range(rounds):
        carry = jnp.zeros((device_count, LANES), F32)
        for u in range(per_round):
            t = r * per_round + u
            holder = lax.div(picks[t : t + 1, :], point_count)
            held = (holder == device_ids).astype(F32)
            running = jnp.dot(held.astype(BF16), lower, preferred_element_type=F32) + carry
            carry = carry + jnp.dot(held.astype(BF16), ones, preferred_element_type=F32)
            rank = jnp.sum(held * running, axis=0, keepdims=True).astype(jnp.int32) - 1
            block = jnp.sum(jnp.where(holders == holder, device_ids, 0), axis=0, keepdims=True)
            place = block * slots + r * cap + rank
            place_ref[t : t + 1, :] = place
            high = lax.div(place, LANES) == iota((slot_chunks, LANES), 0)
            low = (lax.rem(place, LANES) == lane_rows).astype(F32).astype(BF16)
            tag = owner_ref[first_chunk + t : first_chunk + t + 1, :] + 1
            coarse = jnp.where(high, lax.div(tag, 32).astype(F32), 0.0)
            fine = jnp.where(high, lax.rem(tag, 32).astype(F32), 0.0)
            owners = owners + nt_dot(jnp.concatenate([coarse, fine], axis=0).astype(BF16), low)
    slot_owner_ref[...] = (owners[:slot_chunks] * 32.0 + owners[slot_chunks:]).astype(jnp.int32) - 1


def scan_rows(points, piece, best):
    wide = piece.astype(F32)
    half = 0.5 * jnp.sum(wide * wide, axis=1, keepdims=True)
    score = nt_dot(piece, points) - half
    for k in range(0, piece.shape[0], 8):
        best = jnp.maximum(best, score[k : k + 8, :])
    return best


def scan_table(points_ref, table_ref, rows, best):
    points = points_ref[...]
    step = min(256, rows)
    if rows <= 4096:
        for start in range(0, rows, step):
            best = scan_rows(points, table_ref[start : start + step, :], best)
        return best

    def visit(i, best):
        return scan_rows(points, table_ref[pl.ds(pl.multiple_of(i * step, step), step), :], best)

    return lax.fori_loop(0, rows // step, visit, best)


def first_scan_kernel(points_ref, centres_ref, best_ref, norm_ref, token_ref):
    token_ref[...] = jnp.zeros(token_ref.shape, F32)
    best_ref[...] = scan_table(points_ref, centres_ref, centres_ref.shape[0], jnp.full(best_ref.shape, -jnp.inf, F32))
    wide = points_ref[...].astype(F32)
    square = wide * wide
    top = square.astype(BF16)
    rest = (square - top.astype(F32)).astype(BF16)
    ones = jnp.ones((8, square.shape[1]), BF16)
    norm_ref[...] = nt_dot(ones, top) + nt_dot(ones, rest)


def own_scan_kernel(slot_args, rows, points_ref, best_ref, picks_ref, owner_ref, piece_ref, *refs):
    next_ref, count_ref, place_ref, slot_owner_ref, token_ref = refs
    next_ref[...] = scan_table(points_ref, piece_ref, rows, best_ref[...])
    count_ref[...] = add_tally(jnp.zeros(count_ref.shape, F32), piece_ref[rows:, :])
    slot_kernel(*slot_args, picks_ref, owner_ref, place_ref, slot_owner_ref, token_ref)


def next_scan_kernel(rows, tallied, points_ref, best_ref, count_ref, *refs):
    next_ref, next_count_ref, token_ref = refs[-3:]
    token_ref[...] = jnp.zeros(token_ref.shape, F32)
    best, count = best_ref[...], count_ref[...]
    for piece_ref in refs[:-3]:
        best = scan_table(points_ref, piece_ref, rows, best)
        if tallied:
            count = add_tally(count, piece_ref[rows:, :])
    next_ref[...] = best
    next_count_ref[...] = count


def last_scan_kernel(rows, points_ref, best_ref, norm_ref, piece_ref, near_ref, share_ref):
    best = scan_table(points_ref, piece_ref, rows, best_ref[...])
    near = jnp.maximum(norm_ref[0:1, :] - 2.0 * jnp.max(best, axis=0, keepdims=True), 0.0)
    near_ref[...] = near
    share_ref[...] = jnp.broadcast_to(jnp.sum(near, axis=1, keepdims=True)[None], share_ref.shape)


def lloyd_kernel(piece_rows, untold, count_ref, owner_ref, place_ref, slot_owner_ref, centres_ref, *refs):
    piece_refs, out_ref = refs[:-1], refs[-1]
    finals = out_ref.shape[0]
    slot_chunks = slot_owner_ref.shape[0]
    chunks = place_ref.shape[0]
    first_chunks = owner_ref.shape[0] - chunks
    count = count_ref[...]
    for k in untold:
        count = add_tally(count, piece_refs[k][piece_rows:, :])
    weights = 1.0 + count
    weight_top = weights.astype(BF16).astype(F32)
    weight_rest = (weights - weight_top).astype(BF16).astype(F32)
    lane_rows = iota((LANES, LANES), 0)
    placed = jnp.zeros((2 * slot_chunks, LANES), F32)
    for t in range(chunks):
        place = place_ref[t : t + 1, :]
        high = lax.div(place, LANES) == iota((slot_chunks, LANES), 0)
        low = (lax.rem(place, LANES) == lane_rows).astype(F32).astype(BF16)
        c = first_chunks + t
        both = [jnp.where(high, w[c : c + 1, :], 0.0) for w in (weight_top, weight_rest)]
        placed = placed + nt_dot(jnp.concatenate(both, axis=0).astype(BF16), low)
    targets = iota((finals, LANES), 0) + lax.axis_index("row") * finals

    def members(owners, tops, rests, mass):
        parts = []
        for b in range(owners.shape[0]):
            mine = owners[b : b + 1, :] == targets
            top = jnp.where(mine, tops[b : b + 1, :], 0.0)
            rest = jnp.where(mine, rests[b : b + 1, :], 0.0)
            mass = mass + (top + rest)
            parts.append(jnp.concatenate([top, rest], axis=0).astype(BF16))
        return jnp.concatenate(parts, axis=1), mass

    mass = jnp.zeros((finals, LANES), F32)
    member, mass = members(owner_ref[:first_chunks, :], weight_top[:first_chunks], weight_rest[:first_chunks], mass)
    total = jnp.dot(member, centres_ref[...], preferred_element_type=F32)
    start = 0
    for piece_ref in piece_refs:
        rows = piece_ref[:piece_rows, :]
        stop = start + rows.shape[0] // LANES
        member, mass = members(
            slot_owner_ref[start:stop, :], placed[start:stop], placed[slot_chunks + start : slot_chunks + stop], mass
        )
        total = total + jnp.dot(member, rows, preferred_element_type=F32)
        start = stop
    out_ref[...] = (total[:finals] + total[finals:]) / jnp.sum(mass, axis=1, keepdims=True)


def finish_kernel(total_points, near_ref, share_ref, relative_ref):
    cost = jnp.sum(share_ref[...], axis=0)[0:1, 0:1]
    relative_ref[...] = near_ref[...] * total_points / cost


def permute(value, masks):
    pairs = [(d, d ^ masks[(d // CORE) % 2]) for d in range(lax.axis_size(AXES))]
    return lax.ppermute(value, AXES, pairs)


def hop(index):
    masks = tuple(zip(*FAN)) + tuple(zip(*SPREAD))
    return masks[index]


def done_after(value, *tokens):
    ready = tokens[0] >= 0.0
    for token in tokens[1:]:
        ready = ready & (token >= 0.0)
    return jnp.where(ready[:, : value.shape[1]], value, jnp.zeros_like(value))


def both_hops(first, second):
    return tuple(a ^ b for a, b in zip(first, second))


def shards(points, centres, picks, assign_pts, cand_assign):
    point_count, feature_count = points.shape
    row_count, col_count = lax.axis_size("row"), lax.axis_size("col")
    device_count = row_count * col_count
    doubling = (row_count, col_count) == (8, 4)
    round_count, sample_count = picks.shape
    cand_count = centres.shape[0] + round_count * sample_count
    cap = min(point_count, sample_count, -(-2 * sample_count // device_count))
    slots = -(-round_count * cap // 16) * 16
    slot_chunks = device_count * slots // LANES
    chunks = round_count * sample_count // LANES
    finals = K_FINAL // row_count
    shape = jax.ShapeDtypeStruct

    token = shape((1, feature_count), F32)
    id_rows = point_count // LANES
    block_rows = slots + -(-id_rows // 16) * 16
    piece_rows = slots * (4 if doubling else device_count)
    block = local_call(
        functools.partial(pick_kernel, cap, slots),
        shape((block_rows, feature_count), BF16),
        (picks, points, assign_pts.reshape(id_rows, LANES)),
        "pick_rows",
        0.8,
        unread=(0, 1, 2),
        scratch=(
            pltpu.VMEM(picks.shape, jnp.int32),
            pltpu.VMEM(points.shape, BF16),
            pltpu.VMEM((id_rows, LANES), jnp.int32),
            pltpu.SemaphoreType.DMA((3,)),
        ),
    )
    count_shape = shape((cand_count // LANES, LANES), F32)
    owner_rows = cand_assign.reshape(-1, LANES)

    slot_shapes = (shape((chunks, LANES), jnp.int32), shape((slot_chunks, LANES), jnp.int32))

    def find_slots():
        results = (*slot_shapes, token)
        kernel = functools.partial(slot_kernel, doubling, cap, slots, device_count, point_count)
        return local_call(kernel, results, (picks, owner_rows), "slot_owners", 1.0)

    best_shape = shape((8, point_count), F32)

    best, norms, scanned = local_call(
        first_scan_kernel, (best_shape, best_shape, token), (points, centres), "scan_centres", 1.6
    )

    def next_scan(best, counts, tallied, *pieces):
        cost = 0.1 + 0.8e-3 * sum(p.shape[0] for p in pieces)
        kernel = functools.partial(next_scan_kernel, piece_rows, tallied)
        results = (best_shape, count_shape, token)
        return local_call(kernel, results, (points, best, counts, *pieces), "scan_sampled", cost)

    def last_scan(best, piece):
        cost = 0.5 + 0.8e-3 * piece_rows
        kernel = functools.partial(last_scan_kernel, piece_rows)
        results = (shape((1, point_count), F32), shape((device_count, 1, LANES), F32))
        return local_call(kernel, results, (points, best, norms, piece), "scan_last", cost)

    if doubling:
        swap = (CORE, CORE)
        near = [block, *(permute(block, m) for m in (hop(0), hop(1), both_hops(hop(0), hop(1))))]
        own = [part[:slots] for part in near] + [part[slots : slots + id_rows] for part in near]
        own = done_after(jnp.concatenate(own, axis=0), scanned)
        first = permute(own, hop(2))
        second = permute(own, hop(3))
        swapped = [permute(own, swap)]
        best, counts, places, slot_owners, scanned = local_call(
            functools.partial(own_scan_kernel, (doubling, cap, slots, device_count, point_count), piece_rows),
            (best_shape, count_shape, *slot_shapes, token),
            (points, best, picks, owner_rows, own),
            "scan_own",
            1.5,
        )
        third = permute(done_after(first, scanned), hop(3))
        swapped += [permute(first, swap), permute(second, swap)]
        best, counts, scanned = next_scan(best, counts, True, first, second, *swapped)
        swapped.append(permute(done_after(third, scanned), swap))
        best, counts, scanned = next_scan(best, counts, False, third)
        near, share = last_scan(best, swapped[3])
        shares = lax.all_to_all(share, AXES, 0, 0)
        pieces = (own, first, second, third, *swapped)
        untold = (3, 7)
    else:
        places, slot_owners, found = find_slots()
        counts = local_call(tally_kernel, count_shape, (block[slots : slots + id_rows],), "tally", 0.3)
        counts = lax.psum(counts, AXES)
        pieces = (lax.all_gather(block[:slots], AXES, tiled=True),)
        near, share = last_scan(best, pieces[0])
        shares = lax.psum(share[:1], AXES)
        untold = ()
    new_centres = local_call(
        functools.partial(lloyd_kernel, piece_rows, untold),
        shape((finals, feature_count), F32),
        (counts, owner_rows, places, slot_owners, centres, *pieces),
        "lloyd",
        2.6,
    )
    relative = local_call(
        functools.partial(finish_kernel, float(point_count * device_count)),
        shape((1, point_count), F32),
        (near, shares),
        "finish",
        0.6,
    )
    return (relative.reshape(-1), new_centres)


def solution(mesh):
    placed = (P(AXES, None), P(), P(), P(AXES), P())
    return jax.shard_map(
        shards,
        mesh=mesh,
        in_specs=placed,
        out_specs=(P(AXES), P("row", None)),
        check_vma=False,
    )
```

```python
import functools

import jax
import jax.numpy as jnp
from jax import lax
from jax.experimental import pallas as pl
from jax.experimental.pallas import tpu as pltpu
from jax.sharding import PartitionSpec as P

K_FINAL = 1024
AXES = ("row", "col")
LANES = 128
VMEM_LIMIT = 20 * 1024 * 1024
FLOPS_PER_US = 1.0e9
F32 = jnp.float32
BF16 = jnp.bfloat16

CORE = 4
FAN = ((2, 3), (24, 16))
SPREAD = ((24, 16), (2, 3))


def nt_dot(left, right):
    return lax.dot_general(left, right, (((1,), (1,)), ((), ())), preferred_element_type=F32)


def iota(shape, axis):
    return lax.broadcasted_iota(jnp.int32, shape, axis)


def device_index():
    return lax.axis_index("row") * lax.axis_size("col") + lax.axis_index("col")


def whole_spec():
    return pl.BlockSpec(memory_space=pltpu.VMEM)


def local_call(kernel, out_shape, operands, name, cost, after=(), unread=(), scratch=(), passed=(), vmem=VMEM_LIMIT):
    untouched = pl.BlockSpec(memory_space=pl.ANY)
    specs = [whole_spec()] * len(operands) + [untouched] * (len(after) + len(passed))
    result_specs = jax.tree.map(lambda _: whole_spec(), out_shape)
    aliases = {}
    if passed:
        first = len(operands) + len(after)
        aliases = {first + i: len(out_shape) + i for i in range(len(passed))}
        out_shape = (*out_shape, *(jax.ShapeDtypeStruct(x.shape, x.dtype) for x in passed))
        result_specs = (*result_specs, *[untouched] * len(passed))
    operands = list(operands)
    for place in unread:
        specs[place] = pl.BlockSpec(memory_space=pltpu.HBM)
        operands[place] = pltpu.with_memory_space_constraint(operands[place], pltpu.HBM)
    count = len(operands)

    skipped = len(after) + len(passed)
    results = len(out_shape) if isinstance(out_shape, tuple) else 1

    def body(*refs):
        outs = refs[count + skipped : count + skipped + results - len(passed)]
        kernel(*refs[:count], *outs, *refs[count + skipped + results :])

    return pl.pallas_call(
        body,
        out_shape=out_shape,
        in_specs=specs,
        out_specs=result_specs,
        input_output_aliases=aliases,
        scratch_shapes=list(scratch),
        compiler_params=pltpu.CompilerParams(vmem_limit_bytes=vmem),
        cost_estimate=pl.CostEstimate(flops=int(cost * FLOPS_PER_US), bytes_accessed=0, transcendentals=0),
        name=name,
    )(*operands, *after, *passed)


def chunk_rows(ref):
    rounds, samples = ref.shape
    return jnp.concatenate(
        [ref[r : r + 1, k : k + LANES] for r in range(rounds) for k in range(0, samples, LANES)], axis=0
    )


FAR = 2.0**64


def pick_kernel(cap, slots, picks_hbm, points_hbm, assign_hbm, out_ref, points_ref, picks_ref, assign_ref, sems):
    picks_copy = pltpu.make_async_copy(picks_hbm, picks_ref, sems.at[0])
    assign_copy = pltpu.make_async_copy(assign_hbm, assign_ref, sems.at[1])
    points_copy = pltpu.make_async_copy(points_hbm, points_ref, sems.at[2])
    picks_copy.start()
    assign_copy.start()
    points_copy.start()
    picks_copy.wait()
    rounds = picks_ref.shape[0]
    per_round = picks_ref.shape[1] // LANES
    chunks = rounds * per_round
    point_count = points_ref.shape[0]
    local = chunk_rows(picks_ref) - device_index() * point_count
    owned = (local >= 0) & (local < point_count)
    flags = owned.astype(F32).astype(BF16)
    lower = (iota((LANES, LANES), 0) <= iota((LANES, LANES), 1)).astype(F32).astype(BF16)
    inside = jnp.dot(flags, lower, preferred_element_type=F32)
    sums = jnp.dot(flags, jnp.ones((LANES, LANES), BF16), preferred_element_type=F32)
    first, second = iota((chunks, chunks), 0), iota((chunks, chunks), 1)
    same = lax.div(first, per_round) == lax.div(second, per_round)
    earlier = (same & (second < first)).astype(F32).astype(BF16)
    before = jnp.dot(earlier, sums.astype(BF16), preferred_element_type=F32)
    round_of = lax.div(iota((chunks, LANES), 0), per_round)
    slot = (inside + before).astype(jnp.int32) - 1 + round_of * cap
    slot = jnp.where(owned, slot, -1)
    slot_ids = iota((slots, LANES), 0)
    found = jnp.zeros((slots, LANES), jnp.int32)
    for t in range(chunks):
        found = found + jnp.where(slot[t : t + 1, :] == slot_ids, local[t : t + 1, :] + 1, 0)
    place = jnp.sum(found.astype(F32), axis=1, keepdims=True).astype(jnp.int32)
    chosen = (iota((slots, point_count), 1) + 1 == place).astype(F32).astype(BF16)
    assign_copy.wait()
    count = split_counts(tally(assign_ref[...], out_ref.shape[0] - slots))
    points_copy.wait()
    rows = jnp.dot(chosen, points_ref[...], preferred_element_type=F32)
    rows = jnp.where(place > 0, rows, FAR)
    out_ref[...] = jnp.concatenate([rows, count], axis=0).astype(BF16)


def tally(ids, cand_chunks):
    lane_rows = iota((LANES, LANES), 0)
    chunk_ids = iota((cand_chunks, LANES), 0)
    high = [(lax.div(ids[t : t + 1, :], LANES) == chunk_ids).astype(F32) for t in range(ids.shape[0])]
    low = [(lax.rem(ids[t : t + 1, :], LANES) == lane_rows).astype(F32) for t in range(ids.shape[0])]
    return nt_dot(jnp.concatenate(high, axis=1).astype(BF16), jnp.concatenate(low, axis=1).astype(BF16))


def split_counts(count):
    firsts = jnp.floor(count * (1.0 / 256.0))
    return jnp.concatenate([firsts, count - 256.0 * firsts], axis=1)


def join_counts(parts):
    parts = parts.astype(F32)
    return 256.0 * parts[:, :LANES] + parts[:, LANES:]


def holders_in_order(doubling, device_ids):
    if not doubling:
        return device_ids
    me = device_index()
    core = lax.rem(lax.div(me, CORE), 2)
    other = lax.div(device_ids, 16)
    kind = core ^ other
    mask = other * CORE
    for bit, masks in enumerate((*zip(*FAN), *zip(*SPREAD))):
        present = lax.rem(lax.div(device_ids, 1 << bit), 2)
        mask = mask ^ (present * jnp.where(kind == 0, masks[0], masks[1]))
    return me ^ mask


def slot_kernel(doubling, cap, slots, device_count, point_count, picks_ref, owner_ref, place_ref, slot_owner_ref, token_ref):
    token_ref[...] = jnp.zeros(token_ref.shape, F32)
    picks = chunk_rows(picks_ref)
    chunks = picks.shape[0]
    rounds = picks_ref.shape[0]
    per_round = chunks // rounds
    cand_chunks = owner_ref.shape[0]
    slot_chunks = slot_owner_ref.shape[0]
    lane_rows = iota((LANES, LANES), 0)
    lower = (lane_rows <= iota((LANES, LANES), 1)).astype(F32).astype(BF16)
    ones = jnp.ones((LANES, LANES), BF16)
    device_ids = iota((device_count, LANES), 0)
    first_chunk = cand_chunks - chunks
    holders = holders_in_order(doubling, device_ids)
    owners = jnp.zeros((2 * slot_chunks, LANES), F32)
    for r in range(rounds):
        carry = jnp.zeros((device_count, LANES), F32)
        for u in range(per_round):
            t = r * per_round + u
            holder = lax.div(picks[t : t + 1, :], point_count)
            held = (holder == device_ids).astype(F32)
            running = jnp.dot(held.astype(BF16), lower, preferred_element_type=F32) + carry
            carry = carry + jnp.dot(held.astype(BF16), ones, preferred_element_type=F32)
            rank = jnp.sum(held * running, axis=0, keepdims=True).astype(jnp.int32) - 1
            block = jnp.sum(jnp.where(holders == holder, device_ids, 0), axis=0, keepdims=True)
            place = block * slots + r * cap + rank
            place_ref[t : t + 1, :] = place
            high = lax.div(place, LANES) == iota((slot_chunks, LANES), 0)
            low = (lax.rem(place, LANES) == lane_rows).astype(F32).astype(BF16)
            tag = owner_ref[first_chunk + t : first_chunk + t + 1, :] + 1
            coarse = jnp.where(high, lax.div(tag, 32).astype(F32), 0.0)
            fine = jnp.where(high, lax.rem(tag, 32).astype(F32), 0.0)
            owners = owners + nt_dot(jnp.concatenate([coarse, fine], axis=0).astype(BF16), low)
    slot_owner_ref[...] = (owners[:slot_chunks] * 32.0 + owners[slot_chunks:]).astype(jnp.int32) - 1


def scan_rows(points, piece, best):
    wide = piece.astype(F32)
    half = 0.5 * jnp.sum(wide * wide, axis=1, keepdims=True)
    score = nt_dot(piece, points) - half
    for k in range(0, piece.shape[0], 8):
        best = jnp.maximum(best, score[k : k + 8, :])
    return best


def scan_table(points_ref, table_ref, first, rows, best):
    points = points_ref[...]
    step = min(256, rows)
    if rows <= 4096:
        for start in range(first, first + rows, step):
            best = scan_rows(points, table_ref[start : start + step, :], best)
        return best

    def visit(i, best):
        return scan_rows(points, table_ref[pl.ds(pl.multiple_of(i * step, step), step), :], best)

    return lax.fori_loop(0, rows // step, visit, best)


def first_scan_kernel(points_ref, centres_ref, best_ref, norm_ref, token_ref):
    token_ref[...] = jnp.zeros(token_ref.shape, F32)
    best_ref[...] = scan_table(points_ref, centres_ref, 0, centres_ref.shape[0], jnp.full(best_ref.shape, -jnp.inf, F32))
    wide = points_ref[...].astype(F32)
    square = wide * wide
    top = square.astype(BF16)
    rest = (square - top.astype(F32)).astype(BF16)
    ones = jnp.ones((8, square.shape[1]), BF16)
    norm_ref[...] = nt_dot(ones, top) + nt_dot(ones, rest)


def scan_pieces(points_ref, piece_refs, rows, best):
    for piece_ref in piece_refs:
        best = scan_table(points_ref, piece_ref, 0, rows, best)
    return best


def own_scan_kernel(slot_args, rows, points_ref, beside_ref, best_ref, picks_ref, owner_ref, piece_ref, *refs):
    next_ref, beside_best_ref, place_ref, slot_owner_ref, token_ref = refs
    next_ref[...] = scan_pieces(points_ref, [piece_ref], rows, best_ref[...])
    lowest = jnp.full(beside_best_ref.shape, -jnp.inf, F32)
    beside_best_ref[...] = scan_pieces(beside_ref, [piece_ref], rows, lowest)
    slot_kernel(*slot_args, picks_ref, owner_ref, place_ref, slot_owner_ref, token_ref)


def beside_scan_kernel(rows, beside_ref, best_ref, *refs):
    piece_refs, (message_ref, token_ref) = refs[:-2], refs[-2:]
    token_ref[...] = jnp.zeros(token_ref.shape, F32)
    best = scan_pieces(beside_ref, piece_refs[1:], rows, best_ref[...])
    top = jnp.max(best, axis=0, keepdims=True)
    top = [top[:, k : k + LANES] for k in range(0, top.shape[1], LANES)]
    count = join_counts(piece_refs[0][rows:, :])
    for piece_ref in piece_refs[1:]:
        count = count + join_counts(piece_ref[rows:, :])
    message_ref[...] = jnp.concatenate([*top, count], axis=0)


def next_scan_kernel(rows, points_ref, best_ref, start_ref, *refs):
    refs[-1][...] = jnp.max(scan_pieces(points_ref, refs[:-1], rows, best_ref[...]), axis=0, keepdims=True)


def near_kernel(norm_ref, top_ref, message_ref, near_ref, share_ref):
    top = top_ref[...]
    if message_ref is not None:
        told = message_ref[: top.shape[1] // LANES, :]
        top = jnp.maximum(top, jnp.concatenate([told[k : k + 1, :] for k in range(told.shape[0])], axis=1))
    near = jnp.maximum(norm_ref[0:1, :] - 2.0 * top, 0.0)
    near_ref[...] = near
    share_ref[...] = jnp.broadcast_to(jnp.sum(near, axis=1, keepdims=True)[None], share_ref.shape)


def lloyd_kernel(piece_rows, sides, first_place, count_refs, owner_ref, place_ref, slot_owner_ref, centres_ref, *refs):
    piece_refs, out_refs = refs[:-sides], refs[-sides:]
    finals, features = out_refs[0].shape[0], centres_ref.shape[1]
    slot_chunks = slot_owner_ref.shape[0]
    chunks = place_ref.shape[0]
    first_chunks = owner_ref.shape[0] - chunks
    count = sum(ref[first_place:, :] for ref in count_refs)
    weights = 1.0 + count
    weight_top = weights.astype(BF16).astype(F32)
    weight_rest = (weights - weight_top).astype(BF16).astype(F32)
    lane_rows = iota((LANES, LANES), 0)
    placed = jnp.zeros((2 * slot_chunks, LANES), F32)
    for t in range(chunks):
        place = place_ref[t : t + 1, :]
        high = lax.div(place, LANES) == iota((slot_chunks, LANES), 0)
        low = (lax.rem(place, LANES) == lane_rows).astype(F32).astype(BF16)
        c = first_chunks + t
        both = [jnp.where(high, w[c : c + 1, :], 0.0) for w in (weight_top, weight_rest)]
        placed = placed + nt_dot(jnp.concatenate(both, axis=0).astype(BF16), low)
    row = lax.axis_index("row")
    side = lax.rem(row, sides)
    place = iota((sides * finals, LANES), 0)
    targets = place + row * finals
    if sides == 2:
        targets = jnp.where(place < finals, targets, targets - finals + (1 - 2 * side) * finals)

    def members(owners, tops, rests, mass):
        parts = []
        for b in range(owners.shape[0]):
            mine = owners[b : b + 1, :] == targets
            top = jnp.where(mine, tops[b : b + 1, :], 0.0)
            rest = jnp.where(mine, rests[b : b + 1, :], 0.0)
            mass = mass + (top + rest)
            parts.append(jnp.concatenate([top, rest], axis=0).astype(BF16))
        return jnp.concatenate(parts, axis=1), mass

    def share(values):
        height = first_chunks // sides
        return values[:height] if sides == 1 else jnp.where(side == 0, values[:height], values[height : 2 * height])

    mass = jnp.zeros((sides * finals, LANES), F32)
    member, mass = members(share(owner_ref[...]), share(weight_top), share(weight_rest), mass)
    height = centres_ref.shape[0] // sides
    table = centres_ref[pl.ds(pl.multiple_of(side * height, height), height), :]
    total = jnp.dot(member, table, preferred_element_type=F32)
    start = 0
    for piece_ref in piece_refs:
        stop = start + piece_rows // LANES
        member, mass = members(
            slot_owner_ref[start:stop, :], placed[start:stop], placed[slot_chunks + start : slot_chunks + stop], mass
        )
        total = total + jnp.dot(member, piece_ref[:piece_rows, :], preferred_element_type=F32)
        start = stop
    total = total[: sides * finals] + total[sides * finals :]
    for k, out_ref in enumerate(out_refs):
        out_ref[:, :features] = total[k * finals : (k + 1) * finals]
        out_ref[:, features:] = mass[k * finals : (k + 1) * finals]


def centre_kernel(*refs):
    part_refs, (out_ref, token_ref) = refs[:-2], refs[-2:]
    token_ref[...] = jnp.zeros(token_ref.shape, F32)
    features = out_ref.shape[1]
    total = sum(ref[:, :features] for ref in part_refs)
    out_ref[...] = total / jnp.sum(sum(ref[:, features:] for ref in part_refs), axis=1, keepdims=True)


def finish_kernel(total_points, near_ref, share_ref, token_ref, relative_ref):
    cost = jnp.sum(share_ref[...], axis=0)[0:1, 0:1]
    relative_ref[...] = near_ref[...] * total_points / cost


def permute(value, masks):
    pairs = [(d, d ^ masks[(d // CORE) % 2]) for d in range(lax.axis_size(AXES))]
    return lax.ppermute(value, AXES, pairs)


def hop(index):
    masks = tuple(zip(*FAN)) + tuple(zip(*SPREAD))
    return masks[index]


def done_after(value, *tokens):
    ready = tokens[0] >= 0.0
    for token in tokens[1:]:
        ready = ready & (token >= 0.0)
    return jnp.where(ready[:, : value.shape[1]], value, jnp.zeros_like(value))


def both_hops(first, second):
    return tuple(a ^ b for a, b in zip(first, second))


def shards(points, centres, picks, assign_pts, cand_assign):
    point_count, feature_count = points.shape
    row_count, col_count = lax.axis_size("row"), lax.axis_size("col")
    device_count = row_count * col_count
    doubling = (row_count, col_count) == (8, 4)
    round_count, sample_count = picks.shape
    cand_count = centres.shape[0] + round_count * sample_count
    cap = min(point_count, sample_count, -(-2 * sample_count // device_count))
    slots = -(-round_count * cap // 16) * 16
    slot_chunks = device_count * slots // LANES
    chunks = round_count * sample_count // LANES
    finals = K_FINAL // row_count
    shape = jax.ShapeDtypeStruct

    token = shape((1, feature_count), F32)
    cand_chunks = cand_count // LANES
    piece_rows = slots * (4 if doubling else device_count)
    block, near_points = local_call(
        functools.partial(pick_kernel, cap, slots),
        (shape((slots + cand_chunks, feature_count), BF16), shape(points.shape, BF16)),
        (picks, points, assign_pts.reshape(-1, LANES)),
        "pick_rows",
        0.8,
        unread=(0, 1, 2),
        scratch=(
            pltpu.VMEM(picks.shape, jnp.int32),
            pltpu.VMEM((point_count // LANES, LANES), jnp.int32),
            pltpu.SemaphoreType.DMA((3,)),
        ),
    )
    owner_rows = cand_assign.reshape(-1, LANES)
    best_shape = shape((8, point_count), F32)
    top_shape = shape((1, point_count), F32)
    held_chunks = slot_chunks // 2 if doubling else slot_chunks
    slot_shapes = (shape((chunks, LANES), jnp.int32), shape((held_chunks, LANES), jnp.int32))
    slot_args = (doubling, cap, slots, device_count, point_count)
    beside = permute(near_points, (CORE, CORE)) if doubling else near_points
    best, norms, scanned = local_call(
        first_scan_kernel, (best_shape, best_shape, token), (near_points, centres), "scan_centres", 1.6
    )

    def next_scan(points, best, start, *pieces):
        cost = 0.2 + 0.8e-3 * piece_rows * len(pieces)
        kernel = functools.partial(next_scan_kernel, piece_rows)
        return local_call(kernel, top_shape, (points, best, start, *pieces), "scan_next", cost)

    near_shapes = (top_shape, shape((device_count, 1, LANES), F32))
    sum_shape = shape((finals, feature_count + LANES), F32)

    def centres_of(parts):
        return local_call(
            centre_kernel, (shape((finals, feature_count), F32), token), parts, "new_centres", 0.5
        )

    if doubling:
        swap = (CORE, CORE)
        near = [block, *(permute(block, m) for m in (hop(0), hop(1), both_hops(hop(0), hop(1))))]
        told = split_counts(sum(join_counts(part[slots:]) for part in near)).astype(BF16)
        own = done_after(jnp.concatenate([part[:slots] for part in near] + [told], axis=0), scanned)
        others = [permute(own, m) for m in (hop(2), hop(3), both_hops(hop(2), hop(3)))]
        best, beside_best, places, slot_owners, scanned = local_call(
            functools.partial(own_scan_kernel, slot_args, piece_rows),
            (best_shape, best_shape, *slot_shapes, token),
            (near_points, beside, best, picks, owner_rows, own),
            "scan_own",
            2.0,
        )
        message, scanned = local_call(
            functools.partial(beside_scan_kernel, piece_rows),
            (shape((point_count // LANES + cand_chunks, LANES), F32), token),
            (beside, beside_best, own, *others),
            "scan_beside",
            1.2,
        )
        answer = permute(message, swap)
        top = next_scan(near_points, best, scanned, *others)
        near, share = local_call(near_kernel, near_shapes, (norms, top, answer), "nearest", 0.5)
        shares = lax.all_to_all(share, AXES, 0, 0)

        def both_sides(near_ref, mine_ref, other_ref, *refs):
            lloyd_kernel(piece_rows, 2, point_count // LANES, (mine_ref, other_ref), *refs)

        def sum_up(*operands):
            keep, give = local_call(both_sides, (sum_shape, sum_shape), operands, "lloyd", 1.8)
            return centres_of((keep, permute(give, swap)))

        def nothing(*operands):
            return jnp.zeros((finals, feature_count), F32), jnp.zeros(token.shape, F32)

        operands = (near, message, answer, owner_rows, places, slot_owners, centres, own, *others)
        new_centres, summed = lax.cond(lax.axis_index("row") < K_FINAL, sum_up, nothing, *operands)
    else:
        places, slot_owners, found = local_call(
            functools.partial(slot_kernel, *slot_args), (*slot_shapes, token), (picks, owner_rows), "slot_owners", 1.0
        )
        counts = lax.psum(join_counts(block[slots:]), AXES)
        table = lax.all_gather(block[:slots], AXES, tiled=True)
        top = next_scan(near_points, best, scanned, table)

        def nearest(norm_ref, top_ref, *refs):
            near_kernel(norm_ref, top_ref, None, *refs)

        near, share = local_call(nearest, near_shapes, (norms, top), "nearest", 0.5)
        shares = lax.psum(share[:1], AXES)

        def one_side(count_ref, *refs):
            lloyd_kernel(piece_rows, 1, 0, (count_ref,), *refs)

        operands = (counts, owner_rows, places, slot_owners, centres, table)
        new_centres, summed = centres_of((local_call(one_side, sum_shape, operands, "lloyd", 1.8),))
    relative = local_call(
        functools.partial(finish_kernel, float(point_count * device_count)),
        shape((1, point_count), F32),
        (near, shares, summed),
        "finish",
        0.6,
    )
    return (relative.reshape(-1), new_centres)


def solution(mesh):
    placed = (P(AXES, None), P(), P(), P(AXES), P())
    return jax.shard_map(
        shards,
        mesh=mesh,
        in_specs=placed,
        out_specs=(P(AXES), P("row", None)),
        check_vma=False,
    )
```

```python
import functools

import jax
import jax.numpy as jnp
from jax import lax
from jax.experimental import pallas as pl
from jax.experimental.pallas import tpu as pltpu
from jax.sharding import PartitionSpec as P

K_FINAL = 1024
AXES = ("row", "col")
LANES = 128
VMEM_LIMIT = 20 * 1024 * 1024
FLOPS_PER_US = 1.0e9
F32 = jnp.float32
BF16 = jnp.bfloat16

CORE = 4
FAN = ((1, 2), (8, 16))
SPREAD = ((24, 16), (2, 3))


def nt_dot(left, right):
    return lax.dot_general(left, right, (((1,), (1,)), ((), ())), preferred_element_type=F32)


def iota(shape, axis):
    return lax.broadcasted_iota(jnp.int32, shape, axis)


def device_index():
    return lax.axis_index("row") * lax.axis_size("col") + lax.axis_index("col")


def whole_spec():
    return pl.BlockSpec(memory_space=pltpu.VMEM)


def local_call(kernel, out_shape, operands, name, cost, after=(), unread=(), scratch=(), passed=(), vmem=VMEM_LIMIT):
    untouched = pl.BlockSpec(memory_space=pl.ANY)
    specs = [whole_spec()] * len(operands) + [untouched] * (len(after) + len(passed))
    result_specs = jax.tree.map(lambda _: whole_spec(), out_shape)
    aliases = {}
    if passed:
        first = len(operands) + len(after)
        aliases = {first + i: len(out_shape) + i for i in range(len(passed))}
        out_shape = (*out_shape, *(jax.ShapeDtypeStruct(x.shape, x.dtype) for x in passed))
        result_specs = (*result_specs, *[untouched] * len(passed))
    operands = list(operands)
    for place in unread:
        specs[place] = pl.BlockSpec(memory_space=pltpu.HBM)
        operands[place] = pltpu.with_memory_space_constraint(operands[place], pltpu.HBM)
    count = len(operands)

    skipped = len(after) + len(passed)
    results = len(out_shape) if isinstance(out_shape, tuple) else 1

    def body(*refs):
        outs = refs[count + skipped : count + skipped + results - len(passed)]
        kernel(*refs[:count], *outs, *refs[count + skipped + results :])

    return pl.pallas_call(
        body,
        out_shape=out_shape,
        in_specs=specs,
        out_specs=result_specs,
        input_output_aliases=aliases,
        scratch_shapes=list(scratch),
        compiler_params=pltpu.CompilerParams(vmem_limit_bytes=vmem),
        cost_estimate=pl.CostEstimate(flops=int(cost * FLOPS_PER_US), bytes_accessed=0, transcendentals=0),
        name=name,
    )(*operands, *after, *passed)


def chunk_rows(ref):
    rounds, samples = ref.shape
    return jnp.concatenate(
        [ref[r : r + 1, k : k + LANES] for r in range(rounds) for k in range(0, samples, LANES)], axis=0
    )


FAR = 2.0**64


def pick_kernel(cap, slots, picks_hbm, points_hbm, assign_hbm, out_ref, points_ref, picks_ref, assign_ref, sems):
    picks_copy = pltpu.make_async_copy(picks_hbm, picks_ref, sems.at[0])
    assign_copy = pltpu.make_async_copy(assign_hbm, assign_ref, sems.at[1])
    points_copy = pltpu.make_async_copy(points_hbm, points_ref, sems.at[2])
    picks_copy.start()
    assign_copy.start()
    points_copy.start()
    picks_copy.wait()
    rounds = picks_ref.shape[0]
    per_round = picks_ref.shape[1] // LANES
    chunks = rounds * per_round
    point_count = points_ref.shape[0]
    local = chunk_rows(picks_ref) - device_index() * point_count
    owned = (local >= 0) & (local < point_count)
    flags = owned.astype(F32).astype(BF16)
    lower = (iota((LANES, LANES), 0) <= iota((LANES, LANES), 1)).astype(F32).astype(BF16)
    inside = jnp.dot(flags, lower, preferred_element_type=F32)
    sums = jnp.dot(flags, jnp.ones((LANES, LANES), BF16), preferred_element_type=F32)
    first, second = iota((chunks, chunks), 0), iota((chunks, chunks), 1)
    same = lax.div(first, per_round) == lax.div(second, per_round)
    earlier = (same & (second < first)).astype(F32).astype(BF16)
    before = jnp.dot(earlier, sums.astype(BF16), preferred_element_type=F32)
    round_of = lax.div(iota((chunks, LANES), 0), per_round)
    slot = (inside + before).astype(jnp.int32) - 1 + round_of * cap
    slot = jnp.where(owned, slot, -1)
    slot_ids = iota((slots, LANES), 0)
    found = jnp.zeros((slots, LANES), jnp.int32)
    for t in range(chunks):
        found = found + jnp.where(slot[t : t + 1, :] == slot_ids, local[t : t + 1, :] + 1, 0)
    place = jnp.sum(found.astype(F32), axis=1, keepdims=True).astype(jnp.int32)
    chosen = (iota((slots, point_count), 1) + 1 == place).astype(F32).astype(BF16)
    assign_copy.wait()
    count = split_counts(tally(assign_ref[...], out_ref.shape[0] - slots))
    points_copy.wait()
    rows = jnp.dot(chosen, points_ref[...], preferred_element_type=F32)
    rows = jnp.where(place > 0, rows, FAR)
    out_ref[...] = jnp.concatenate([rows, count], axis=0).astype(BF16)


def tally(ids, cand_chunks):
    lane_rows = iota((LANES, LANES), 0)
    chunk_ids = iota((cand_chunks, LANES), 0)
    high = [(lax.div(ids[t : t + 1, :], LANES) == chunk_ids).astype(F32) for t in range(ids.shape[0])]
    low = [(lax.rem(ids[t : t + 1, :], LANES) == lane_rows).astype(F32) for t in range(ids.shape[0])]
    return nt_dot(jnp.concatenate(high, axis=1).astype(BF16), jnp.concatenate(low, axis=1).astype(BF16))


def split_counts(count):
    firsts = jnp.floor(count * (1.0 / 256.0))
    return jnp.concatenate([firsts, count - 256.0 * firsts], axis=1)


def join_counts(parts):
    parts = parts.astype(F32)
    return 256.0 * parts[:, :LANES] + parts[:, LANES:]


def holders_in_order(doubling, device_ids):
    if not doubling:
        return device_ids
    me = device_index()
    core = lax.rem(lax.div(me, CORE), 2)
    other = lax.div(device_ids, 16)
    kind = core ^ other
    mask = other * CORE
    for bit, masks in enumerate((*zip(*FAN), *zip(*SPREAD))):
        present = lax.rem(lax.div(device_ids, 1 << bit), 2)
        mask = mask ^ (present * jnp.where(kind == 0, masks[0], masks[1]))
    return me ^ mask


def slot_kernel(doubling, cap, slots, device_count, point_count, picks_ref, owner_ref, place_ref, slot_owner_ref, token_ref):
    token_ref[...] = jnp.zeros(token_ref.shape, F32)
    picks = chunk_rows(picks_ref)
    chunks = picks.shape[0]
    rounds = picks_ref.shape[0]
    per_round = chunks // rounds
    cand_chunks = owner_ref.shape[0]
    slot_chunks = slot_owner_ref.shape[0]
    lane_rows = iota((LANES, LANES), 0)
    lower = (lane_rows <= iota((LANES, LANES), 1)).astype(F32).astype(BF16)
    ones = jnp.ones((LANES, LANES), BF16)
    device_ids = iota((device_count, LANES), 0)
    first_chunk = cand_chunks - chunks
    holders = holders_in_order(doubling, device_ids)
    owners = jnp.zeros((2 * slot_chunks, LANES), F32)
    for r in range(rounds):
        carry = jnp.zeros((device_count, LANES), F32)
        for u in range(per_round):
            t = r * per_round + u
            holder = lax.div(picks[t : t + 1, :], point_count)
            held = (holder == device_ids).astype(F32)
            running = jnp.dot(held.astype(BF16), lower, preferred_element_type=F32) + carry
            carry = carry + jnp.dot(held.astype(BF16), ones, preferred_element_type=F32)
            rank = jnp.sum(held * running, axis=0, keepdims=True).astype(jnp.int32) - 1
            block = jnp.sum(jnp.where(holders == holder, device_ids, 0), axis=0, keepdims=True)
            place = block * slots + r * cap + rank
            place_ref[t : t + 1, :] = place
            high = lax.div(place, LANES) == iota((slot_chunks, LANES), 0)
            low = (lax.rem(place, LANES) == lane_rows).astype(F32).astype(BF16)
            tag = owner_ref[first_chunk + t : first_chunk + t + 1, :] + 1
            coarse = jnp.where(high, lax.div(tag, 32).astype(F32), 0.0)
            fine = jnp.where(high, lax.rem(tag, 32).astype(F32), 0.0)
            owners = owners + nt_dot(jnp.concatenate([coarse, fine], axis=0).astype(BF16), low)
    slot_owner_ref[...] = (owners[:slot_chunks] * 32.0 + owners[slot_chunks:]).astype(jnp.int32) - 1


def scan_rows(points, piece, best):
    wide = piece.astype(F32)
    half = 0.5 * jnp.sum(wide * wide, axis=1, keepdims=True)
    score = nt_dot(piece, points) - half
    for k in range(0, piece.shape[0], 8):
        best = jnp.maximum(best, score[k : k + 8, :])
    return best


def scan_table(points_ref, table_ref, first, rows, best):
    points = points_ref[...]
    step = min(256, rows)
    if rows <= 4096:
        for start in range(first, first + rows, step):
            best = scan_rows(points, table_ref[start : start + step, :], best)
        return best

    def visit(i, best):
        return scan_rows(points, table_ref[pl.ds(pl.multiple_of(i * step, step), step), :], best)

    return lax.fori_loop(0, rows // step, visit, best)


def first_scan_kernel(points_ref, centres_ref, best_ref, norm_ref):
    best_ref[...] = scan_table(points_ref, centres_ref, 0, centres_ref.shape[0], jnp.full(best_ref.shape, -jnp.inf, F32))
    wide = points_ref[...].astype(F32)
    square = wide * wide
    top = square.astype(BF16)
    rest = (square - top.astype(F32)).astype(BF16)
    ones = jnp.ones((8, square.shape[1]), BF16)
    norm_ref[...] = nt_dot(ones, top) + nt_dot(ones, rest)


def scan_pieces(points_ref, piece_refs, rows, best):
    for piece_ref in piece_refs:
        best = scan_table(points_ref, piece_ref, 0, rows, best)
    return best


def own_scan_kernel(slot_args, rows, points_ref, centres_ref, picks_ref, owner_ref, piece_ref, *refs):
    best_ref, norm_ref, place_ref, slot_owner_ref, token_ref = refs
    first_scan_kernel(points_ref, centres_ref, best_ref, norm_ref)
    best_ref[...] = scan_pieces(points_ref, [piece_ref], rows, best_ref[...])
    slot_kernel(*slot_args, picks_ref, owner_ref, place_ref, slot_owner_ref, token_ref)


def start_scan_kernel(rows, beside_ref, piece_ref, best_ref):
    best_ref[...] = scan_pieces(beside_ref, [piece_ref], rows, jnp.full(best_ref.shape, -jnp.inf, F32))


def beside_scan_kernel(rows, beside_ref, best_ref, *refs):
    piece_refs, (message_ref, token_ref) = refs[:-2], refs[-2:]
    token_ref[...] = jnp.zeros(token_ref.shape, F32)
    best = scan_pieces(beside_ref, piece_refs[1:], rows, best_ref[...])
    top = jnp.max(best, axis=0, keepdims=True)
    top = [top[:, k : k + LANES] for k in range(0, top.shape[1], LANES)]
    count = join_counts(piece_refs[0][rows:, :])
    for piece_ref in piece_refs[1:]:
        count = count + join_counts(piece_ref[rows:, :])
    message_ref[...] = jnp.concatenate([*top, count], axis=0)


def next_scan_kernel(rows, points_ref, best_ref, start_ref, *refs):
    refs[-1][...] = jnp.max(scan_pieces(points_ref, refs[:-1], rows, best_ref[...]), axis=0, keepdims=True)


def near_kernel(norm_ref, top_ref, message_ref, near_ref, share_ref):
    top = top_ref[...]
    if message_ref is not None:
        told = message_ref[: top.shape[1] // LANES, :]
        top = jnp.maximum(top, jnp.concatenate([told[k : k + 1, :] for k in range(told.shape[0])], axis=1))
    near = jnp.maximum(norm_ref[0:1, :] - 2.0 * top, 0.0)
    near_ref[...] = near
    share_ref[...] = jnp.broadcast_to(jnp.sum(near, axis=1, keepdims=True)[None], share_ref.shape)


def lloyd_kernel(piece_rows, sides, first_place, count_refs, owner_ref, place_ref, slot_owner_ref, centres_ref, *refs):
    piece_refs, out_refs = refs[:-sides], refs[-sides:]
    finals, features = out_refs[0].shape[0], centres_ref.shape[1]
    slot_chunks = slot_owner_ref.shape[0]
    chunks = place_ref.shape[0]
    first_chunks = owner_ref.shape[0] - chunks
    count = sum(ref[first_place:, :] for ref in count_refs)
    weights = 1.0 + count
    weight_top = weights.astype(BF16).astype(F32)
    weight_rest = (weights - weight_top).astype(BF16).astype(F32)
    lane_rows = iota((LANES, LANES), 0)
    placed = jnp.zeros((2 * slot_chunks, LANES), F32)
    for t in range(chunks):
        place = place_ref[t : t + 1, :]
        high = lax.div(place, LANES) == iota((slot_chunks, LANES), 0)
        low = (lax.rem(place, LANES) == lane_rows).astype(F32).astype(BF16)
        c = first_chunks + t
        both = [jnp.where(high, w[c : c + 1, :], 0.0) for w in (weight_top, weight_rest)]
        placed = placed + nt_dot(jnp.concatenate(both, axis=0).astype(BF16), low)
    row = lax.axis_index("row")
    side = lax.rem(row, sides)
    place = iota((sides * finals, LANES), 0)
    targets = place + row * finals
    if sides == 2:
        targets = jnp.where(place < finals, targets, targets - finals + (1 - 2 * side) * finals)

    def members(owners, tops, rests, mass):
        parts = []
        for b in range(owners.shape[0]):
            mine = owners[b : b + 1, :] == targets
            top = jnp.where(mine, tops[b : b + 1, :], 0.0)
            rest = jnp.where(mine, rests[b : b + 1, :], 0.0)
            mass = mass + (top + rest)
            parts.append(jnp.concatenate([top, rest], axis=0).astype(BF16))
        return jnp.concatenate(parts, axis=1), mass

    def share(values):
        height = first_chunks // sides
        return values[:height] if sides == 1 else jnp.where(side == 0, values[:height], values[height : 2 * height])

    mass = jnp.zeros((sides * finals, LANES), F32)
    member, mass = members(share(owner_ref[...]), share(weight_top), share(weight_rest), mass)
    height = centres_ref.shape[0] // sides
    table = centres_ref[pl.ds(pl.multiple_of(side * height, height), height), :]
    total = jnp.dot(member, table, preferred_element_type=F32)
    start = 0
    for piece_ref in piece_refs:
        stop = start + piece_rows // LANES
        member, mass = members(
            slot_owner_ref[start:stop, :], placed[start:stop], placed[slot_chunks + start : slot_chunks + stop], mass
        )
        total = total + jnp.dot(member, piece_ref[:piece_rows, :], preferred_element_type=F32)
        start = stop
    total = total[: sides * finals] + total[sides * finals :]
    for k, out_ref in enumerate(out_refs):
        out_ref[:, :features] = total[k * finals : (k + 1) * finals]
        out_ref[:, features:] = mass[k * finals : (k + 1) * finals]


def centre_kernel(*refs):
    part_refs, (out_ref, token_ref) = refs[:-2], refs[-2:]
    token_ref[...] = jnp.zeros(token_ref.shape, F32)
    features = out_ref.shape[1]
    total = sum(ref[:, :features] for ref in part_refs)
    out_ref[...] = total / jnp.sum(sum(ref[:, features:] for ref in part_refs), axis=1, keepdims=True)


def finish_kernel(total_points, near_ref, share_ref, token_ref, relative_ref):
    cost = jnp.sum(share_ref[...], axis=0)[0:1, 0:1]
    relative_ref[...] = near_ref[...] * total_points / cost


def permute(value, masks):
    pairs = [(d, d ^ masks[(d // CORE) % 2]) for d in range(lax.axis_size(AXES))]
    return lax.ppermute(value, AXES, pairs)


def hop(index):
    masks = tuple(zip(*FAN)) + tuple(zip(*SPREAD))
    return masks[index]


def done_after(value, *tokens):
    ready = tokens[0] >= 0.0
    for token in tokens[1:]:
        ready = ready & (token >= 0.0)
    return jnp.where(ready[:, : value.shape[1]], value, jnp.zeros_like(value))


def both_hops(first, second):
    return tuple(a ^ b for a, b in zip(first, second))


def shards(points, centres, picks, assign_pts, cand_assign):
    point_count, feature_count = points.shape
    row_count, col_count = lax.axis_size("row"), lax.axis_size("col")
    device_count = row_count * col_count
    doubling = (row_count, col_count) == (8, 4)
    round_count, sample_count = picks.shape
    cand_count = centres.shape[0] + round_count * sample_count
    cap = min(point_count, sample_count, -(-2 * sample_count // device_count))
    slots = -(-round_count * cap // 16) * 16
    slot_chunks = device_count * slots // LANES
    chunks = round_count * sample_count // LANES
    finals = K_FINAL // row_count
    shape = jax.ShapeDtypeStruct

    token = shape((1, feature_count), F32)
    cand_chunks = cand_count // LANES
    piece_rows = slots * (4 if doubling else device_count)
    block, near_points = local_call(
        functools.partial(pick_kernel, cap, slots),
        (shape((slots + cand_chunks, feature_count), BF16), shape(points.shape, BF16)),
        (picks, points, assign_pts.reshape(-1, LANES)),
        "pick_rows",
        0.8,
        unread=(0, 1, 2),
        scratch=(
            pltpu.VMEM(picks.shape, jnp.int32),
            pltpu.VMEM((point_count // LANES, LANES), jnp.int32),
            pltpu.SemaphoreType.DMA((3,)),
        ),
    )
    owner_rows = cand_assign.reshape(-1, LANES)
    best_shape = shape((8, point_count), F32)
    top_shape = shape((1, point_count), F32)
    held_chunks = slot_chunks // 2 if doubling else slot_chunks
    slot_shapes = (shape((chunks, LANES), jnp.int32), shape((held_chunks, LANES), jnp.int32))
    slot_args = (doubling, cap, slots, device_count, point_count)
    def next_scan(points, best, start, *pieces):
        cost = 0.2 + 0.8e-3 * piece_rows * len(pieces)
        kernel = functools.partial(next_scan_kernel, piece_rows)
        return local_call(kernel, top_shape, (points, best, start, *pieces), "scan_next", cost)

    near_shapes = (top_shape, shape((device_count, 1, LANES), F32))
    sum_shape = shape((finals, feature_count + LANES), F32)

    def centres_of(parts):
        return local_call(
            centre_kernel, (shape((finals, feature_count), F32), token), parts, "new_centres", 0.5
        )

    if doubling:
        swap = (CORE, CORE)
        near = [block, *(permute(block, m) for m in (hop(0), hop(1), both_hops(hop(0), hop(1))))]
        told = split_counts(sum(join_counts(part[slots:]) for part in near)).astype(BF16)
        own = jnp.concatenate([part[:slots] for part in near] + [told], axis=0)
        others = [permute(own, m) for m in (hop(2), hop(3), both_hops(hop(2), hop(3)))]
        best, norms, places, slot_owners, scanned = local_call(
            functools.partial(own_scan_kernel, slot_args, piece_rows),
            (best_shape, best_shape, *slot_shapes, token),
            (near_points, centres, picks, owner_rows, own),
            "scan_own",
            3.0,
        )
        beside = permute(near_points, swap)
        beside_best = local_call(
            functools.partial(start_scan_kernel, piece_rows), best_shape, (beside, own), "scan_start", 0.5
        )
        message, scanned = local_call(
            functools.partial(beside_scan_kernel, piece_rows),
            (shape((point_count // LANES + cand_chunks, LANES), F32), token),
            (beside, beside_best, own, *others),
            "scan_beside",
            1.2,
        )
        answer = permute(message, swap)
        top = next_scan(near_points, best, scanned, *others)
        near, share = local_call(near_kernel, near_shapes, (norms, top, answer), "nearest", 0.5)
        shares = lax.all_to_all(share, AXES, 0, 0)

        def both_sides(near_ref, mine_ref, other_ref, *refs):
            lloyd_kernel(piece_rows, 2, point_count // LANES, (mine_ref, other_ref), *refs)

        def sum_up(*operands):
            keep, give = local_call(both_sides, (sum_shape, sum_shape), operands, "lloyd", 1.8)
            return centres_of((keep, permute(give, swap)))

        def nothing(*operands):
            return jnp.zeros((finals, feature_count), F32), jnp.zeros(token.shape, F32)

        operands = (near, message, answer, owner_rows, places, slot_owners, centres, own, *others)
        new_centres, summed = lax.cond(lax.axis_index("row") < K_FINAL, sum_up, nothing, *operands)
    else:
        best, norms = local_call(
            first_scan_kernel, (best_shape, best_shape), (near_points, centres), "scan_centres", 1.6
        )
        places, slot_owners, found = local_call(
            functools.partial(slot_kernel, *slot_args), (*slot_shapes, token), (picks, owner_rows), "slot_owners", 1.0
        )
        counts = lax.psum(join_counts(block[slots:]), AXES)
        table = lax.all_gather(block[:slots], AXES, tiled=True)
        top = next_scan(near_points, best, found, table)

        def nearest(norm_ref, top_ref, *refs):
            near_kernel(norm_ref, top_ref, None, *refs)

        near, share = local_call(nearest, near_shapes, (norms, top), "nearest", 0.5)
        shares = lax.psum(share[:1], AXES)

        def one_side(count_ref, *refs):
            lloyd_kernel(piece_rows, 1, 0, (count_ref,), *refs)

        operands = (counts, owner_rows, places, slot_owners, centres, table)
        new_centres, summed = centres_of((local_call(one_side, sum_shape, operands, "lloyd", 1.8),))
    relative = local_call(
        functools.partial(finish_kernel, float(point_count * device_count)),
        shape((1, point_count), F32),
        (near, shares, summed),
        "finish",
        0.6,
    )
    return (relative.reshape(-1), new_centres)


def solution(mesh):
    placed = (P(AXES, None), P(), P(), P(AXES), P())
    return jax.shard_map(
        shards,
        mesh=mesh,
        in_specs=placed,
        out_specs=(P(AXES), P("row", None)),
        check_vma=False,
    )
```

```python
import functools

import jax
import jax.numpy as jnp
from jax import lax
from jax.experimental import pallas as pl
from jax.experimental.pallas import tpu as pltpu
from jax.sharding import PartitionSpec as P

K_FINAL = 1024
AXES = ("row", "col")
LANES = 128
VMEM_LIMIT = 20 * 1024 * 1024
FLOPS_PER_US = 1.0e9
F32 = jnp.float32
BF16 = jnp.bfloat16

CORE = 4
FAN = ((3, 2), (24, 16))
SPREAD = ((24, 16), (2, 3))


def nt_dot(left, right):
    return lax.dot_general(left, right, (((1,), (1,)), ((), ())), preferred_element_type=F32)


def iota(shape, axis):
    return lax.broadcasted_iota(jnp.int32, shape, axis)


def device_index():
    return lax.axis_index("row") * lax.axis_size("col") + lax.axis_index("col")


def whole_spec():
    return pl.BlockSpec(memory_space=pltpu.VMEM)


def local_call(kernel, out_shape, operands, name, cost, after=(), unread=(), scratch=(), passed=(), vmem=VMEM_LIMIT):
    untouched = pl.BlockSpec(memory_space=pl.ANY)
    specs = [whole_spec()] * len(operands) + [untouched] * (len(after) + len(passed))
    result_specs = jax.tree.map(lambda _: whole_spec(), out_shape)
    aliases = {}
    if passed:
        first = len(operands) + len(after)
        aliases = {first + i: len(out_shape) + i for i in range(len(passed))}
        out_shape = (*out_shape, *(jax.ShapeDtypeStruct(x.shape, x.dtype) for x in passed))
        result_specs = (*result_specs, *[untouched] * len(passed))
    operands = list(operands)
    for place in unread:
        specs[place] = pl.BlockSpec(memory_space=pltpu.HBM)
        operands[place] = pltpu.with_memory_space_constraint(operands[place], pltpu.HBM)
    count = len(operands)

    skipped = len(after) + len(passed)
    results = len(out_shape) if isinstance(out_shape, tuple) else 1

    def body(*refs):
        outs = refs[count + skipped : count + skipped + results - len(passed)]
        kernel(*refs[:count], *outs, *refs[count + skipped + results :])

    return pl.pallas_call(
        body,
        out_shape=out_shape,
        in_specs=specs,
        out_specs=result_specs,
        input_output_aliases=aliases,
        scratch_shapes=list(scratch),
        compiler_params=pltpu.CompilerParams(vmem_limit_bytes=vmem),
        cost_estimate=pl.CostEstimate(flops=int(cost * FLOPS_PER_US), bytes_accessed=0, transcendentals=0),
        name=name,
    )(*operands, *after, *passed)


def chunk_rows(ref):
    rounds, samples = ref.shape
    return jnp.concatenate(
        [ref[r : r + 1, k : k + LANES] for r in range(rounds) for k in range(0, samples, LANES)], axis=0
    )


FAR = 2.0**64


def pick_kernel(cap, slots, picks_hbm, points_hbm, assign_hbm, out_ref, points_ref, picks_ref, assign_ref, sems):
    picks_copy = pltpu.make_async_copy(picks_hbm, picks_ref, sems.at[0])
    assign_copy = pltpu.make_async_copy(assign_hbm, assign_ref, sems.at[1])
    points_copy = pltpu.make_async_copy(points_hbm, points_ref, sems.at[2])
    picks_copy.start()
    assign_copy.start()
    points_copy.start()
    picks_copy.wait()
    rounds = picks_ref.shape[0]
    per_round = picks_ref.shape[1] // LANES
    chunks = rounds * per_round
    point_count = points_ref.shape[0]
    local = chunk_rows(picks_ref) - device_index() * point_count
    owned = (local >= 0) & (local < point_count)
    flags = owned.astype(F32).astype(BF16)
    lower = (iota((LANES, LANES), 0) <= iota((LANES, LANES), 1)).astype(F32).astype(BF16)
    inside = jnp.dot(flags, lower, preferred_element_type=F32)
    sums = jnp.dot(flags, jnp.ones((LANES, LANES), BF16), preferred_element_type=F32)
    first, second = iota((chunks, chunks), 0), iota((chunks, chunks), 1)
    same = lax.div(first, per_round) == lax.div(second, per_round)
    earlier = (same & (second < first)).astype(F32).astype(BF16)
    before = jnp.dot(earlier, sums.astype(BF16), preferred_element_type=F32)
    round_of = lax.div(iota((chunks, LANES), 0), per_round)
    slot = (inside + before).astype(jnp.int32) - 1 + round_of * cap
    slot = jnp.where(owned, slot, -1)
    slot_ids = iota((slots, LANES), 0)
    found = jnp.zeros((slots, LANES), jnp.int32)
    for t in range(chunks):
        found = found + jnp.where(slot[t : t + 1, :] == slot_ids, local[t : t + 1, :] + 1, 0)
    place = jnp.sum(found.astype(F32), axis=1, keepdims=True).astype(jnp.int32)
    chosen = (iota((slots, point_count), 1) + 1 == place).astype(F32).astype(BF16)
    assign_copy.wait()
    count = split_counts(tally(assign_ref[...], out_ref.shape[0] - slots))
    points_copy.wait()
    rows = jnp.dot(chosen, points_ref[...], preferred_element_type=F32)
    rows = jnp.where(place > 0, rows, FAR)
    out_ref[...] = jnp.concatenate([rows, count], axis=0).astype(BF16)


def tally(ids, cand_chunks):
    lane_rows = iota((LANES, LANES), 0)
    chunk_ids = iota((cand_chunks, LANES), 0)
    high = [(lax.div(ids[t : t + 1, :], LANES) == chunk_ids).astype(F32) for t in range(ids.shape[0])]
    low = [(lax.rem(ids[t : t + 1, :], LANES) == lane_rows).astype(F32) for t in range(ids.shape[0])]
    return nt_dot(jnp.concatenate(high, axis=1).astype(BF16), jnp.concatenate(low, axis=1).astype(BF16))


def split_counts(count):
    firsts = jnp.floor(count * (1.0 / 256.0))
    return jnp.concatenate([firsts, count - 256.0 * firsts], axis=1)


def join_counts(parts):
    parts = parts.astype(F32)
    return 256.0 * parts[:, :LANES] + parts[:, LANES:]


def holders_in_order(doubling, device_ids):
    if not doubling:
        return device_ids
    me = device_index()
    core = lax.rem(lax.div(me, CORE), 2)
    other = lax.div(device_ids, 16)
    kind = core ^ other
    mask = other * CORE
    for bit, masks in enumerate((*zip(*FAN), *zip(*SPREAD))):
        present = lax.rem(lax.div(device_ids, 1 << bit), 2)
        mask = mask ^ (present * jnp.where(kind == 0, masks[0], masks[1]))
    return me ^ mask


def slot_kernel(doubling, cap, slots, device_count, point_count, picks_ref, owner_ref, place_ref, slot_owner_ref, token_ref):
    token_ref[...] = jnp.zeros(token_ref.shape, F32)
    picks = chunk_rows(picks_ref)
    chunks = picks.shape[0]
    rounds = picks_ref.shape[0]
    per_round = chunks // rounds
    cand_chunks = owner_ref.shape[0]
    slot_chunks = slot_owner_ref.shape[0]
    lane_rows = iota((LANES, LANES), 0)
    lower = (lane_rows <= iota((LANES, LANES), 1)).astype(F32).astype(BF16)
    ones = jnp.ones((LANES, LANES), BF16)
    device_ids = iota((device_count, LANES), 0)
    first_chunk = cand_chunks - chunks
    holders = holders_in_order(doubling, device_ids)
    owners = jnp.zeros((2 * slot_chunks, LANES), F32)
    for r in range(rounds):
        carry = jnp.zeros((device_count, LANES), F32)
        for u in range(per_round):
            t = r * per_round + u
            holder = lax.div(picks[t : t + 1, :], point_count)
            held = (holder == device_ids).astype(F32)
            running = jnp.dot(held.astype(BF16), lower, preferred_element_type=F32) + carry
            carry = carry + jnp.dot(held.astype(BF16), ones, preferred_element_type=F32)
            rank = jnp.sum(held * running, axis=0, keepdims=True).astype(jnp.int32) - 1
            block = jnp.sum(jnp.where(holders == holder, device_ids, 0), axis=0, keepdims=True)
            place = block * slots + r * cap + rank
            place_ref[t : t + 1, :] = place
            high = lax.div(place, LANES) == iota((slot_chunks, LANES), 0)
            low = (lax.rem(place, LANES) == lane_rows).astype(F32).astype(BF16)
            tag = owner_ref[first_chunk + t : first_chunk + t + 1, :] + 1
            coarse = jnp.where(high, lax.div(tag, 32).astype(F32), 0.0)
            fine = jnp.where(high, lax.rem(tag, 32).astype(F32), 0.0)
            owners = owners + nt_dot(jnp.concatenate([coarse, fine], axis=0).astype(BF16), low)
    slot_owner_ref[...] = (owners[:slot_chunks] * 32.0 + owners[slot_chunks:]).astype(jnp.int32) - 1


def scan_rows(points, piece, best):
    wide = piece.astype(F32)
    half = 0.5 * jnp.sum(wide * wide, axis=1, keepdims=True)
    score = nt_dot(piece, points) - half
    for k in range(0, piece.shape[0], 8):
        best = jnp.maximum(best, score[k : k + 8, :])
    return best


def scan_table(points_ref, table_ref, first, rows, best):
    points = points_ref[...]
    step = min(256, rows)
    if rows <= 4096:
        for start in range(first, first + rows, step):
            best = scan_rows(points, table_ref[start : start + step, :], best)
        return best

    def visit(i, best):
        return scan_rows(points, table_ref[pl.ds(pl.multiple_of(i * step, step), step), :], best)

    return lax.fori_loop(0, rows // step, visit, best)


def first_scan_kernel(points_ref, centres_ref, best_ref, norm_ref):
    best_ref[...] = scan_table(points_ref, centres_ref, 0, centres_ref.shape[0], jnp.full(best_ref.shape, -jnp.inf, F32))
    wide = points_ref[...].astype(F32)
    square = wide * wide
    top = square.astype(BF16)
    rest = (square - top.astype(F32)).astype(BF16)
    ones = jnp.ones((8, square.shape[1]), BF16)
    norm_ref[...] = nt_dot(ones, top) + nt_dot(ones, rest)


def scan_pieces(points_ref, piece_refs, rows, best):
    for piece_ref in piece_refs:
        best = scan_table(points_ref, piece_ref, 0, rows, best)
    return best


def own_scan_kernel(slot_args, rows, points_ref, centres_ref, picks_ref, owner_ref, piece_ref, *refs):
    best_ref, norm_ref, place_ref, slot_owner_ref, token_ref = refs
    first_scan_kernel(points_ref, centres_ref, best_ref, norm_ref)
    best_ref[...] = scan_pieces(points_ref, [piece_ref], rows, best_ref[...])
    slot_kernel(*slot_args, picks_ref, owner_ref, place_ref, slot_owner_ref, token_ref)


def both_scan_kernel(rows, points_ref, beside_ref, best_ref, own_ref, piece_ref, next_ref, beside_best_ref):
    next_ref[...] = scan_pieces(points_ref, [piece_ref], rows, best_ref[...])
    lowest = jnp.full(beside_best_ref.shape, -jnp.inf, F32)
    beside_best_ref[...] = scan_pieces(beside_ref, [own_ref, piece_ref], rows, lowest)


def beside_scan_kernel(rows, beside_ref, best_ref, *refs):
    piece_refs, (message_ref, token_ref) = refs[:-2], refs[-2:]
    token_ref[...] = jnp.zeros(token_ref.shape, F32)
    best = scan_pieces(beside_ref, piece_refs[2:], rows, best_ref[...])
    top = jnp.max(best, axis=0, keepdims=True)
    top = [top[:, k : k + LANES] for k in range(0, top.shape[1], LANES)]
    count = join_counts(piece_refs[0][rows:, :])
    for piece_ref in piece_refs[1:]:
        count = count + join_counts(piece_ref[rows:, :])
    message_ref[...] = jnp.concatenate([*top, count], axis=0)


def next_scan_kernel(rows, points_ref, best_ref, start_ref, *refs):
    refs[-1][...] = jnp.max(scan_pieces(points_ref, refs[:-1], rows, best_ref[...]), axis=0, keepdims=True)


def near_kernel(norm_ref, top_ref, message_ref, near_ref, share_ref):
    top = top_ref[...]
    if message_ref is not None:
        told = message_ref[: top.shape[1] // LANES, :]
        top = jnp.maximum(top, jnp.concatenate([told[k : k + 1, :] for k in range(told.shape[0])], axis=1))
    near = jnp.maximum(norm_ref[0:1, :] - 2.0 * top, 0.0)
    near_ref[...] = near
    share_ref[...] = jnp.broadcast_to(jnp.sum(near, axis=1, keepdims=True)[None], share_ref.shape)


def lloyd_kernel(piece_rows, sides, first_place, count_refs, owner_ref, place_ref, slot_owner_ref, centres_ref, *refs):
    piece_refs, out_refs = refs[:-sides], refs[-sides:]
    finals, features = out_refs[0].shape[0], centres_ref.shape[1]
    slot_chunks = slot_owner_ref.shape[0]
    chunks = place_ref.shape[0]
    first_chunks = owner_ref.shape[0] - chunks
    count = sum(ref[first_place:, :] for ref in count_refs)
    weights = 1.0 + count
    weight_top = weights.astype(BF16).astype(F32)
    weight_rest = (weights - weight_top).astype(BF16).astype(F32)
    lane_rows = iota((LANES, LANES), 0)
    placed = jnp.zeros((2 * slot_chunks, LANES), F32)
    for t in range(chunks):
        place = place_ref[t : t + 1, :]
        high = lax.div(place, LANES) == iota((slot_chunks, LANES), 0)
        low = (lax.rem(place, LANES) == lane_rows).astype(F32).astype(BF16)
        c = first_chunks + t
        both = [jnp.where(high, w[c : c + 1, :], 0.0) for w in (weight_top, weight_rest)]
        placed = placed + nt_dot(jnp.concatenate(both, axis=0).astype(BF16), low)
    row = lax.axis_index("row")
    side = lax.rem(row, sides)
    place = iota((sides * finals, LANES), 0)
    targets = place + row * finals
    if sides == 2:
        targets = jnp.where(place < finals, targets, targets - finals + (1 - 2 * side) * finals)

    def members(owners, tops, rests, mass):
        parts = []
        for b in range(owners.shape[0]):
            mine = owners[b : b + 1, :] == targets
            top = jnp.where(mine, tops[b : b + 1, :], 0.0)
            rest = jnp.where(mine, rests[b : b + 1, :], 0.0)
            mass = mass + (top + rest)
            parts.append(jnp.concatenate([top, rest], axis=0).astype(BF16))
        return jnp.concatenate(parts, axis=1), mass

    def share(values):
        height = first_chunks // sides
        return values[:height] if sides == 1 else jnp.where(side == 0, values[:height], values[height : 2 * height])

    mass = jnp.zeros((sides * finals, LANES), F32)
    member, mass = members(share(owner_ref[...]), share(weight_top), share(weight_rest), mass)
    height = centres_ref.shape[0] // sides
    table = centres_ref[pl.ds(pl.multiple_of(side * height, height), height), :]
    total = jnp.dot(member, table, preferred_element_type=F32)
    start = 0
    for piece_ref in piece_refs:
        stop = start + piece_rows // LANES
        member, mass = members(
            slot_owner_ref[start:stop, :], placed[start:stop], placed[slot_chunks + start : slot_chunks + stop], mass
        )
        total = total + jnp.dot(member, piece_ref[:piece_rows, :], preferred_element_type=F32)
        start = stop
    total = total[: sides * finals] + total[sides * finals :]
    for k, out_ref in enumerate(out_refs):
        out_ref[:, :features] = total[k * finals : (k + 1) * finals]
        out_ref[:, features:] = mass[k * finals : (k + 1) * finals]


def centre_kernel(*refs):
    part_refs, (out_ref, token_ref) = refs[:-2], refs[-2:]
    token_ref[...] = jnp.zeros(token_ref.shape, F32)
    features = out_ref.shape[1]
    total = sum(ref[:, :features] for ref in part_refs)
    out_ref[...] = total / jnp.sum(sum(ref[:, features:] for ref in part_refs), axis=1, keepdims=True)


def finish_kernel(total_points, near_ref, share_ref, token_ref, relative_ref):
    cost = jnp.sum(share_ref[...], axis=0)[0:1, 0:1]
    relative_ref[...] = near_ref[...] * total_points / cost


def permute(value, masks):
    pairs = [(d, d ^ masks[(d // CORE) % 2]) for d in range(lax.axis_size(AXES))]
    return lax.ppermute(value, AXES, pairs)


def hop(index):
    masks = tuple(zip(*FAN)) + tuple(zip(*SPREAD))
    return masks[index]


def done_after(value, *tokens):
    ready = tokens[0] >= 0.0
    for token in tokens[1:]:
        ready = ready & (token >= 0.0)
    return jnp.where(ready[:, : value.shape[1]], value, jnp.zeros_like(value))


def both_hops(first, second):
    return tuple(a ^ b for a, b in zip(first, second))


def shards(points, centres, picks, assign_pts, cand_assign):
    point_count, feature_count = points.shape
    row_count, col_count = lax.axis_size("row"), lax.axis_size("col")
    device_count = row_count * col_count
    doubling = (row_count, col_count) == (8, 4)
    round_count, sample_count = picks.shape
    cand_count = centres.shape[0] + round_count * sample_count
    cap = min(point_count, sample_count, -(-2 * sample_count // device_count))
    slots = -(-round_count * cap // 16) * 16
    slot_chunks = device_count * slots // LANES
    chunks = round_count * sample_count // LANES
    finals = K_FINAL // row_count
    shape = jax.ShapeDtypeStruct

    token = shape((1, feature_count), F32)
    cand_chunks = cand_count // LANES
    piece_rows = slots * (4 if doubling else device_count)
    block, near_points = local_call(
        functools.partial(pick_kernel, cap, slots),
        (shape((slots + cand_chunks, feature_count), BF16), shape(points.shape, BF16)),
        (picks, points, assign_pts.reshape(-1, LANES)),
        "pick_rows",
        0.8,
        unread=(0, 1, 2),
        scratch=(
            pltpu.VMEM(picks.shape, jnp.int32),
            pltpu.VMEM((point_count // LANES, LANES), jnp.int32),
            pltpu.SemaphoreType.DMA((3,)),
        ),
    )
    owner_rows = cand_assign.reshape(-1, LANES)
    best_shape = shape((8, point_count), F32)
    top_shape = shape((1, point_count), F32)
    held_chunks = slot_chunks // 2 if doubling else slot_chunks
    slot_shapes = (shape((chunks, LANES), jnp.int32), shape((held_chunks, LANES), jnp.int32))
    slot_args = (doubling, cap, slots, device_count, point_count)
    def next_scan(points, best, start, *pieces):
        cost = 0.2 + 0.8e-3 * piece_rows * len(pieces)
        kernel = functools.partial(next_scan_kernel, piece_rows)
        return local_call(kernel, top_shape, (points, best, start, *pieces), "scan_next", cost)

    near_shapes = (top_shape, shape((device_count, 1, LANES), F32))
    sum_shape = shape((finals, feature_count + LANES), F32)

    def centres_of(parts):
        return local_call(
            centre_kernel, (shape((finals, feature_count), F32), token), parts, "new_centres", 0.5
        )

    if doubling:
        swap = (CORE, CORE)
        near = [block, *(permute(block, m) for m in (hop(0), hop(1), both_hops(hop(0), hop(1))))]
        told = split_counts(sum(join_counts(part[slots:]) for part in near)).astype(BF16)
        own = jnp.concatenate([part[:slots] for part in near] + [told], axis=0)
        others = [permute(own, m) for m in (hop(2), hop(3), both_hops(hop(2), hop(3)))]
        best, norms, places, slot_owners, scanned = local_call(
            functools.partial(own_scan_kernel, slot_args, piece_rows),
            (best_shape, best_shape, *slot_shapes, token),
            (near_points, centres, picks, owner_rows, own),
            "scan_own",
            3.0,
        )
        beside = permute(near_points, swap)
        best, beside_best = local_call(
            functools.partial(both_scan_kernel, piece_rows),
            (best_shape, best_shape),
            (near_points, beside, best, own, others[0]),
            "scan_both",
            1.3,
        )
        message, scanned = local_call(
            functools.partial(beside_scan_kernel, piece_rows),
            (shape((point_count // LANES + cand_chunks, LANES), F32), token),
            (beside, beside_best, own, *others),
            "scan_beside",
            1.2,
        )
        answer = permute(message, swap)
        top = next_scan(near_points, best, scanned, *others[1:])
        near, share = local_call(near_kernel, near_shapes, (norms, top, answer), "nearest", 0.5)
        shares = lax.all_to_all(share, AXES, 0, 0)

        def both_sides(near_ref, mine_ref, other_ref, *refs):
            lloyd_kernel(piece_rows, 2, point_count // LANES, (mine_ref, other_ref), *refs)

        def sum_up(*operands):
            keep, give = local_call(both_sides, (sum_shape, sum_shape), operands, "lloyd", 1.8)
            return centres_of((keep, permute(give, swap)))

        def nothing(*operands):
            return jnp.zeros((finals, feature_count), F32), jnp.zeros(token.shape, F32)

        operands = (near, message, answer, owner_rows, places, slot_owners, centres, own, *others)
        new_centres, summed = lax.cond(lax.axis_index("row") < K_FINAL, sum_up, nothing, *operands)
    else:
        best, norms = local_call(
            first_scan_kernel, (best_shape, best_shape), (near_points, centres), "scan_centres", 1.6
        )
        places, slot_owners, found = local_call(
            functools.partial(slot_kernel, *slot_args), (*slot_shapes, token), (picks, owner_rows), "slot_owners", 1.0
        )
        counts = lax.psum(join_counts(block[slots:]), AXES)
        table = lax.all_gather(block[:slots], AXES, tiled=True)
        top = next_scan(near_points, best, found, table)

        def nearest(norm_ref, top_ref, *refs):
            near_kernel(norm_ref, top_ref, None, *refs)

        near, share = local_call(nearest, near_shapes, (norms, top), "nearest", 0.5)
        shares = lax.psum(share[:1], AXES)

        def one_side(count_ref, *refs):
            lloyd_kernel(piece_rows, 1, 0, (count_ref,), *refs)

        operands = (counts, owner_rows, places, slot_owners, centres, table)
        new_centres, summed = centres_of((local_call(one_side, sum_shape, operands, "lloyd", 1.8),))
    relative = local_call(
        functools.partial(finish_kernel, float(point_count * device_count)),
        shape((1, point_count), F32),
        (near, shares, summed),
        "finish",
        0.6,
    )
    return (relative.reshape(-1), new_centres)


def solution(mesh):
    placed = (P(AXES, None), P(), P(), P(AXES), P())
    return jax.shard_map(
        shards,
        mesh=mesh,
        in_specs=placed,
        out_specs=(P(AXES), P("row", None)),
        check_vma=False,
    )
```

```python
import functools

import jax
import jax.numpy as jnp
from jax import lax
from jax.experimental import pallas as pl
from jax.experimental.pallas import tpu as pltpu
from jax.sharding import PartitionSpec as P

K_FINAL = 1024
AXES = ("row", "col")
LANES = 128
VMEM_LIMIT = 20 * 1024 * 1024
FLOPS_PER_US = 1.0e9
F32 = jnp.float32
BF16 = jnp.bfloat16

CORE = 4
FAN = ((3, 2), (24, 16))
SPREAD = ((24, 16), (2, 3))


def nt_dot(left, right):
    return lax.dot_general(left, right, (((1,), (1,)), ((), ())), preferred_element_type=F32)


def iota(shape, axis):
    return lax.broadcasted_iota(jnp.int32, shape, axis)


def device_index():
    return lax.axis_index("row") * lax.axis_size("col") + lax.axis_index("col")


def whole_spec():
    return pl.BlockSpec(memory_space=pltpu.VMEM)


def local_call(kernel, out_shape, operands, name, cost, after=(), unread=(), scratch=(), passed=(), vmem=VMEM_LIMIT):
    untouched = pl.BlockSpec(memory_space=pl.ANY)
    specs = [whole_spec()] * len(operands) + [untouched] * (len(after) + len(passed))
    result_specs = jax.tree.map(lambda _: whole_spec(), out_shape)
    aliases = {}
    if passed:
        first = len(operands) + len(after)
        aliases = {first + i: len(out_shape) + i for i in range(len(passed))}
        out_shape = (*out_shape, *(jax.ShapeDtypeStruct(x.shape, x.dtype) for x in passed))
        result_specs = (*result_specs, *[untouched] * len(passed))
    operands = list(operands)
    for place in unread:
        specs[place] = pl.BlockSpec(memory_space=pltpu.HBM)
        operands[place] = pltpu.with_memory_space_constraint(operands[place], pltpu.HBM)
    count = len(operands)

    skipped = len(after) + len(passed)
    results = len(out_shape) if isinstance(out_shape, tuple) else 1

    def body(*refs):
        outs = refs[count + skipped : count + skipped + results - len(passed)]
        kernel(*refs[:count], *outs, *refs[count + skipped + results :])

    return pl.pallas_call(
        body,
        out_shape=out_shape,
        in_specs=specs,
        out_specs=result_specs,
        input_output_aliases=aliases,
        scratch_shapes=list(scratch),
        compiler_params=pltpu.CompilerParams(vmem_limit_bytes=vmem),
        cost_estimate=pl.CostEstimate(flops=int(cost * FLOPS_PER_US), bytes_accessed=0, transcendentals=0),
        name=name,
    )(*operands, *after, *passed)


def chunk_rows(ref):
    rounds, samples = ref.shape
    return jnp.concatenate(
        [ref[r : r + 1, k : k + LANES] for r in range(rounds) for k in range(0, samples, LANES)], axis=0
    )


FAR = 2.0**64


def pick_kernel(cap, slots, picks_hbm, points_hbm, assign_hbm, out_ref, points_ref, picks_ref, assign_ref, sems):
    picks_copy = pltpu.make_async_copy(picks_hbm, picks_ref, sems.at[0])
    assign_copy = pltpu.make_async_copy(assign_hbm, assign_ref, sems.at[1])
    points_copy = pltpu.make_async_copy(points_hbm, points_ref, sems.at[2])
    picks_copy.start()
    assign_copy.start()
    points_copy.start()
    picks_copy.wait()
    rounds = picks_ref.shape[0]
    per_round = picks_ref.shape[1] // LANES
    chunks = rounds * per_round
    point_count = points_ref.shape[0]
    local = chunk_rows(picks_ref) - device_index() * point_count
    owned = (local >= 0) & (local < point_count)
    flags = owned.astype(F32).astype(BF16)
    lower = (iota((LANES, LANES), 0) <= iota((LANES, LANES), 1)).astype(F32).astype(BF16)
    inside = jnp.dot(flags, lower, preferred_element_type=F32)
    sums = jnp.dot(flags, jnp.ones((LANES, LANES), BF16), preferred_element_type=F32)
    first, second = iota((chunks, chunks), 0), iota((chunks, chunks), 1)
    same = lax.div(first, per_round) == lax.div(second, per_round)
    earlier = (same & (second < first)).astype(F32).astype(BF16)
    before = jnp.dot(earlier, sums.astype(BF16), preferred_element_type=F32)
    round_of = lax.div(iota((chunks, LANES), 0), per_round)
    slot = (inside + before).astype(jnp.int32) - 1 + round_of * cap
    slot = jnp.where(owned, slot, -1)
    slot_ids = iota((slots, LANES), 0)
    found = jnp.zeros((slots, LANES), jnp.int32)
    for t in range(chunks):
        found = found + jnp.where(slot[t : t + 1, :] == slot_ids, local[t : t + 1, :] + 1, 0)
    place = jnp.sum(found.astype(F32), axis=1, keepdims=True).astype(jnp.int32)
    chosen = (iota((slots, point_count), 1) + 1 == place).astype(F32).astype(BF16)
    assign_copy.wait()
    ids = assign_ref[...]
    ids = jnp.concatenate([lax.div(ids, LANES), lax.rem(ids, LANES)], axis=1).astype(F32)
    points_copy.wait()
    rows = jnp.dot(chosen, points_ref[...], preferred_element_type=F32)
    rows = jnp.where(place > 0, rows, FAR)
    out_ref[...] = jnp.concatenate([rows, ids], axis=0).astype(BF16)


def add_tally(count, ids):
    lane_rows = iota((LANES, LANES), 0).astype(F32)
    chunk_ids = iota(count.shape, 0).astype(F32)
    ids = ids.astype(F32)
    for start in range(0, ids.shape[0], 8):
        rows = [ids[t : t + 1, :] for t in range(start, start + 8)]
        high = [(row[:, :LANES] == chunk_ids).astype(F32) for row in rows]
        low = [(row[:, LANES:] == lane_rows).astype(F32) for row in rows]
        high = jnp.concatenate(high, axis=1).astype(BF16)
        low = jnp.concatenate(low, axis=1).astype(BF16)
        count = count + nt_dot(high, low)
    return count


def tally_kernel(first, count_ref, *refs):
    count = count_ref[...]
    for ref in refs[:-1]:
        count = add_tally(count, ref[first:, :])
    refs[-1][...] = count


def holders_in_order(doubling, device_ids):
    if not doubling:
        return device_ids
    me = device_index()
    core = lax.rem(lax.div(me, CORE), 2)
    other = lax.div(device_ids, 16)
    kind = core ^ other
    mask = other * CORE
    for bit, masks in enumerate((*zip(*FAN), *zip(*SPREAD))):
        present = lax.rem(lax.div(device_ids, 1 << bit), 2)
        mask = mask ^ (present * jnp.where(kind == 0, masks[0], masks[1]))
    return me ^ mask


def slot_kernel(doubling, cap, slots, device_count, point_count, picks_ref, owner_ref, place_ref, slot_owner_ref, token_ref):
    token_ref[...] = jnp.zeros(token_ref.shape, F32)
    picks = chunk_rows(picks_ref)
    chunks = picks.shape[0]
    rounds = picks_ref.shape[0]
    per_round = chunks // rounds
    cand_chunks = owner_ref.shape[0]
    slot_chunks = slot_owner_ref.shape[0]
    lane_rows = iota((LANES, LANES), 0)
    lower = (lane_rows <= iota((LANES, LANES), 1)).astype(F32).astype(BF16)
    ones = jnp.ones((LANES, LANES), BF16)
    device_ids = iota((device_count, LANES), 0)
    first_chunk = cand_chunks - chunks
    holders = holders_in_order(doubling, device_ids)
    owners = jnp.zeros((2 * slot_chunks, LANES), F32)
    for r in range(rounds):
        carry = jnp.zeros((device_count, LANES), F32)
        for u in range(per_round):
            t = r * per_round + u
            holder = lax.div(picks[t : t + 1, :], point_count)
            held = (holder == device_ids).astype(F32)
            running = jnp.dot(held.astype(BF16), lower, preferred_element_type=F32) + carry
            carry = carry + jnp.dot(held.astype(BF16), ones, preferred_element_type=F32)
            rank = jnp.sum(held * running, axis=0, keepdims=True).astype(jnp.int32) - 1
            block = jnp.sum(jnp.where(holders == holder, device_ids, 0), axis=0, keepdims=True)
            place = block * slots + r * cap + rank
            place_ref[t : t + 1, :] = place
            high = lax.div(place, LANES) == iota((slot_chunks, LANES), 0)
            low = (lax.rem(place, LANES) == lane_rows).astype(F32).astype(BF16)
            tag = owner_ref[first_chunk + t : first_chunk + t + 1, :] + 1
            coarse = jnp.where(high, lax.div(tag, 32).astype(F32), 0.0)
            fine = jnp.where(high, lax.rem(tag, 32).astype(F32), 0.0)
            owners = owners + nt_dot(jnp.concatenate([coarse, fine], axis=0).astype(BF16), low)
    slot_owner_ref[...] = (owners[:slot_chunks] * 32.0 + owners[slot_chunks:]).astype(jnp.int32) - 1


def scan_rows(points, piece, best):
    wide = piece.astype(F32)
    half = 0.5 * jnp.sum(wide * wide, axis=1, keepdims=True)
    score = nt_dot(piece, points) - half
    for k in range(0, piece.shape[0], 8):
        best = jnp.maximum(best, score[k : k + 8, :])
    return best


def scan_table(points_ref, table_ref, first, rows, best):
    points = points_ref[...]
    step = min(256, rows)
    if rows <= 4096:
        for start in range(first, first + rows, step):
            best = scan_rows(points, table_ref[start : start + step, :], best)
        return best

    def visit(i, best):
        return scan_rows(points, table_ref[pl.ds(pl.multiple_of(i * step, step), step), :], best)

    return lax.fori_loop(0, rows // step, visit, best)


def first_scan_kernel(points_ref, centres_ref, best_ref, norm_ref):
    best_ref[...] = scan_table(points_ref, centres_ref, 0, centres_ref.shape[0], jnp.full(best_ref.shape, -jnp.inf, F32))
    wide = points_ref[...].astype(F32)
    square = wide * wide
    top = square.astype(BF16)
    rest = (square - top.astype(F32)).astype(BF16)
    ones = jnp.ones((8, square.shape[1]), BF16)
    norm_ref[...] = nt_dot(ones, top) + nt_dot(ones, rest)


def scan_pieces(points_ref, piece_refs, rows, best):
    for piece_ref in piece_refs:
        best = scan_table(points_ref, piece_ref, 0, rows, best)
    return best


def own_scan_kernel(slot_args, rows, points_ref, centres_ref, picks_ref, owner_ref, piece_ref, *refs):
    best_ref, norm_ref, place_ref, slot_owner_ref, token_ref = refs
    first_scan_kernel(points_ref, centres_ref, best_ref, norm_ref)
    best_ref[...] = scan_pieces(points_ref, [piece_ref], rows, best_ref[...])
    slot_kernel(*slot_args, picks_ref, owner_ref, place_ref, slot_owner_ref, token_ref)


def both_scan_kernel(rows, points_ref, beside_ref, best_ref, own_ref, piece_ref, *refs):
    next_ref, next_count_ref, beside_best_ref = refs
    next_ref[...] = scan_pieces(points_ref, [piece_ref], rows, best_ref[...])
    next_count_ref[...] = add_tally(jnp.zeros(next_count_ref.shape, F32), piece_ref[rows:, :])
    lowest = jnp.full(beside_best_ref.shape, -jnp.inf, F32)
    beside_best_ref[...] = scan_pieces(beside_ref, [own_ref, piece_ref], rows, lowest)


def beside_scan_kernel(rows, beside_ref, best_ref, *refs):
    top_ref, token_ref = refs[-2:]
    token_ref[...] = jnp.zeros(token_ref.shape, F32)
    top_ref[...] = jnp.max(scan_pieces(beside_ref, refs[:-2], rows, best_ref[...]), axis=0, keepdims=True)


def next_scan_kernel(rows, points_ref, best_ref, start_ref, *refs):
    refs[-1][...] = jnp.max(scan_pieces(points_ref, refs[:-1], rows, best_ref[...]), axis=0, keepdims=True)


def near_kernel(norm_ref, top_ref, beside_ref, near_ref, share_ref):
    top = jnp.maximum(top_ref[...], beside_ref[...])
    near = jnp.maximum(norm_ref[0:1, :] - 2.0 * top, 0.0)
    near_ref[...] = near
    share_ref[...] = jnp.broadcast_to(jnp.sum(near, axis=1, keepdims=True)[None], share_ref.shape)


def lloyd_kernel(piece_rows, sides, count_refs, owner_ref, place_ref, slot_owner_ref, centres_ref, *refs):
    piece_refs, out_refs = refs[:-sides], refs[-sides:]
    finals, features = out_refs[0].shape[0], centres_ref.shape[1]
    slot_chunks = slot_owner_ref.shape[0]
    chunks = place_ref.shape[0]
    first_chunks = owner_ref.shape[0] - chunks
    count = sum(ref[...] for ref in count_refs)
    weights = 1.0 + count
    weight_top = weights.astype(BF16).astype(F32)
    weight_rest = (weights - weight_top).astype(BF16).astype(F32)
    lane_rows = iota((LANES, LANES), 0)
    placed = jnp.zeros((2 * slot_chunks, LANES), F32)
    for t in range(chunks):
        place = place_ref[t : t + 1, :]
        high = lax.div(place, LANES) == iota((slot_chunks, LANES), 0)
        low = (lax.rem(place, LANES) == lane_rows).astype(F32).astype(BF16)
        c = first_chunks + t
        both = [jnp.where(high, w[c : c + 1, :], 0.0) for w in (weight_top, weight_rest)]
        placed = placed + nt_dot(jnp.concatenate(both, axis=0).astype(BF16), low)
    row = lax.axis_index("row")
    side = lax.rem(row, sides)
    place = iota((sides * finals, LANES), 0)
    targets = place + row * finals
    if sides == 2:
        targets = jnp.where(place < finals, targets, targets - finals + (1 - 2 * side) * finals)

    def members(owners, tops, rests, mass):
        parts = []
        for b in range(owners.shape[0]):
            mine = owners[b : b + 1, :] == targets
            top = jnp.where(mine, tops[b : b + 1, :], 0.0)
            rest = jnp.where(mine, rests[b : b + 1, :], 0.0)
            mass = mass + (top + rest)
            parts.append(jnp.concatenate([top, rest], axis=0).astype(BF16))
        return jnp.concatenate(parts, axis=1), mass

    def share(values):
        height = first_chunks // sides
        return values[:height] if sides == 1 else jnp.where(side == 0, values[:height], values[height : 2 * height])

    mass = jnp.zeros((sides * finals, LANES), F32)
    member, mass = members(share(owner_ref[...]), share(weight_top), share(weight_rest), mass)
    height = centres_ref.shape[0] // sides
    table = centres_ref[pl.ds(pl.multiple_of(side * height, height), height), :]
    total = jnp.dot(member, table, preferred_element_type=F32)
    start = 0
    for piece_ref in piece_refs:
        stop = start + piece_rows // LANES
        member, mass = members(
            slot_owner_ref[start:stop, :], placed[start:stop], placed[slot_chunks + start : slot_chunks + stop], mass
        )
        total = total + jnp.dot(member, piece_ref[:piece_rows, :], preferred_element_type=F32)
        start = stop
    total = total[: sides * finals] + total[sides * finals :]
    for k, out_ref in enumerate(out_refs):
        out_ref[:, :features] = total[k * finals : (k + 1) * finals]
        out_ref[:, features:] = mass[k * finals : (k + 1) * finals]


def centre_kernel(*refs):
    part_refs, (out_ref, token_ref) = refs[:-2], refs[-2:]
    token_ref[...] = jnp.zeros(token_ref.shape, F32)
    features = out_ref.shape[1]
    total = sum(ref[:, :features] for ref in part_refs)
    out_ref[...] = total / jnp.sum(sum(ref[:, features:] for ref in part_refs), axis=1, keepdims=True)


def finish_kernel(total_points, near_ref, share_ref, token_ref, relative_ref):
    cost = jnp.sum(share_ref[...], axis=0)[0:1, 0:1]
    relative_ref[...] = near_ref[...] * total_points / cost


def permute(value, masks):
    pairs = [(d, d ^ masks[(d // CORE) % 2]) for d in range(lax.axis_size(AXES))]
    return lax.ppermute(value, AXES, pairs)


def hop(index):
    masks = tuple(zip(*FAN)) + tuple(zip(*SPREAD))
    return masks[index]


def done_after(value, *tokens):
    ready = tokens[0] >= 0.0
    for token in tokens[1:]:
        ready = ready & (token >= 0.0)
    return jnp.where(ready[:, : value.shape[1]], value, jnp.zeros_like(value))


def both_hops(first, second):
    return tuple(a ^ b for a, b in zip(first, second))


def shards(points, centres, picks, assign_pts, cand_assign):
    point_count, feature_count = points.shape
    row_count, col_count = lax.axis_size("row"), lax.axis_size("col")
    device_count = row_count * col_count
    doubling = (row_count, col_count) == (8, 4)
    round_count, sample_count = picks.shape
    cand_count = centres.shape[0] + round_count * sample_count
    cap = min(point_count, sample_count, -(-2 * sample_count // device_count))
    slots = -(-round_count * cap // 16) * 16
    slot_chunks = device_count * slots // LANES
    chunks = round_count * sample_count // LANES
    finals = K_FINAL // row_count
    shape = jax.ShapeDtypeStruct

    token = shape((1, feature_count), F32)
    count_shape = shape((cand_count // LANES, LANES), F32)
    id_rows = point_count // LANES
    piece_rows = slots * (4 if doubling else device_count)
    block, near_points = local_call(
        functools.partial(pick_kernel, cap, slots),
        (shape((slots + id_rows, feature_count), BF16), shape(points.shape, BF16)),
        (picks, points, assign_pts.reshape(id_rows, LANES)),
        "pick_rows",
        0.8,
        unread=(0, 1, 2),
        scratch=(
            pltpu.VMEM(picks.shape, jnp.int32),
            pltpu.VMEM((id_rows, LANES), jnp.int32),
            pltpu.SemaphoreType.DMA((3,)),
        ),
    )
    owner_rows = cand_assign.reshape(-1, LANES)
    best_shape = shape((8, point_count), F32)
    top_shape = shape((1, point_count), F32)
    held_chunks = slot_chunks // 2 if doubling else slot_chunks
    slot_shapes = (shape((chunks, LANES), jnp.int32), shape((held_chunks, LANES), jnp.int32))
    slot_args = (doubling, cap, slots, device_count, point_count)
    def next_scan(points, best, start, *pieces):
        cost = 0.2 + 0.8e-3 * piece_rows * len(pieces)
        kernel = functools.partial(next_scan_kernel, piece_rows)
        return local_call(kernel, top_shape, (points, best, start, *pieces), "scan_next", cost)

    near_shapes = (top_shape, shape((device_count, 1, LANES), F32))
    sum_shape = shape((finals, feature_count + LANES), F32)

    def centres_of(parts):
        return local_call(
            centre_kernel, (shape((finals, feature_count), F32), token), parts, "new_centres", 0.5
        )

    if doubling:
        swap = (CORE, CORE)
        near = [block, *(permute(block, m) for m in (hop(0), hop(1), both_hops(hop(0), hop(1))))]
        own = [part[:slots] for part in near] + [part[slots:] for part in near]
        own = jnp.concatenate(own, axis=0)
        others = [permute(own, m) for m in (hop(2), hop(3), both_hops(hop(2), hop(3)))]
        best, norms, places, slot_owners, scanned = local_call(
            functools.partial(own_scan_kernel, slot_args, piece_rows),
            (best_shape, best_shape, *slot_shapes, token),
            (near_points, centres, picks, owner_rows, own),
            "scan_own",
            3.0,
        )
        beside = permute(near_points, swap)
        best, counts, beside_best = local_call(
            functools.partial(both_scan_kernel, piece_rows),
            (best_shape, count_shape, best_shape),
            (near_points, beside, best, own, others[0]),
            "scan_both",
            1.3,
        )
        message, scanned = local_call(
            functools.partial(beside_scan_kernel, piece_rows),
            (top_shape, token),
            (beside, beside_best, *others[1:]),
            "scan_beside",
            0.9,
        )
        answer = permute(message, swap)
        top = next_scan(near_points, best, scanned, *others[1:])
        near, share = local_call(near_kernel, near_shapes, (norms, top, answer), "nearest", 0.5)
        shares = lax.all_to_all(share, AXES, 0, 0)

        def both_sides(mine_ref, other_ref, *refs):
            lloyd_kernel(piece_rows, 2, (mine_ref, other_ref), *refs)

        def rest_of_tally(near_ref, *refs):
            tally_kernel(piece_rows, *refs)

        def sum_up(near, counts, *operands):
            own, *others = operands[-4:]
            counts = local_call(rest_of_tally, count_shape, (near, counts, own, *others[1:]), "tally", 1.2)
            operands = (counts, permute(counts, swap), *operands)
            keep, give = local_call(both_sides, (sum_shape, sum_shape), operands, "lloyd", 1.8)
            return centres_of((keep, permute(give, swap)))

        def nothing(*operands):
            return jnp.zeros((finals, feature_count), F32), jnp.zeros(token.shape, F32)

        operands = (near, counts, owner_rows, places, slot_owners, centres, own, *others)
        new_centres, summed = lax.cond(lax.axis_index("row") < K_FINAL, sum_up, nothing, *operands)
    else:
        best, norms = local_call(
            first_scan_kernel, (best_shape, best_shape), (near_points, centres), "scan_centres", 1.6
        )
        places, slot_owners, found = local_call(
            functools.partial(slot_kernel, *slot_args), (*slot_shapes, token), (picks, owner_rows), "slot_owners", 1.0
        )
        counts = jnp.zeros(count_shape.shape, F32)
        counts = local_call(functools.partial(tally_kernel, 0), count_shape, (counts, block[slots:]), "tally", 0.3)
        counts = lax.psum(counts, AXES)
        table = lax.all_gather(block[:slots], AXES, tiled=True)
        top = next_scan(near_points, best, found, table)

        near, share = local_call(near_kernel, near_shapes, (norms, top, top), "nearest", 0.5)
        shares = lax.psum(share[:1], AXES)

        def one_side(count_ref, *refs):
            lloyd_kernel(piece_rows, 1, (count_ref,), *refs)

        operands = (counts, owner_rows, places, slot_owners, centres, table)
        new_centres, summed = centres_of((local_call(one_side, sum_shape, operands, "lloyd", 1.8),))
    relative = local_call(
        functools.partial(finish_kernel, float(point_count * device_count)),
        shape((1, point_count), F32),
        (near, shares, summed),
        "finish",
        0.6,
    )
    return (relative.reshape(-1), new_centres)


def solution(mesh):
    placed = (P(AXES, None), P(), P(), P(AXES), P())
    return jax.shard_map(
        shards,
        mesh=mesh,
        in_specs=placed,
        out_specs=(P(AXES), P("row", None)),
        check_vma=False,
    )
```

```python
import functools

import jax
import jax.numpy as jnp
from jax import lax
from jax.experimental import pallas as pl
from jax.experimental.pallas import tpu as pltpu
from jax.sharding import PartitionSpec as P

K_FINAL = 1024
AXES = ("row", "col")
LANES = 128
VMEM_LIMIT = 20 * 1024 * 1024
FLOPS_PER_US = 1.0e9
F32 = jnp.float32
BF16 = jnp.bfloat16

CORE = 4
FAN = ((3, 2), (24, 16))
SPREAD = ((24, 16), (3, 2))


def nt_dot(left, right):
    return lax.dot_general(left, right, (((1,), (1,)), ((), ())), preferred_element_type=F32)


def iota(shape, axis):
    return lax.broadcasted_iota(jnp.int32, shape, axis)


def device_index():
    return lax.axis_index("row") * lax.axis_size("col") + lax.axis_index("col")


def whole_spec():
    return pl.BlockSpec(memory_space=pltpu.VMEM)


def local_call(kernel, out_shape, operands, name, cost, after=(), unread=(), scratch=(), passed=(), vmem=VMEM_LIMIT):
    untouched = pl.BlockSpec(memory_space=pl.ANY)
    specs = [whole_spec()] * len(operands) + [untouched] * (len(after) + len(passed))
    result_specs = jax.tree.map(lambda _: whole_spec(), out_shape)
    aliases = {}
    if passed:
        first = len(operands) + len(after)
        aliases = {first + i: len(out_shape) + i for i in range(len(passed))}
        out_shape = (*out_shape, *(jax.ShapeDtypeStruct(x.shape, x.dtype) for x in passed))
        result_specs = (*result_specs, *[untouched] * len(passed))
    operands = list(operands)
    for place in unread:
        specs[place] = pl.BlockSpec(memory_space=pltpu.HBM)
        operands[place] = pltpu.with_memory_space_constraint(operands[place], pltpu.HBM)
    count = len(operands)

    skipped = len(after) + len(passed)
    results = len(out_shape) if isinstance(out_shape, tuple) else 1

    def body(*refs):
        outs = refs[count + skipped : count + skipped + results - len(passed)]
        kernel(*refs[:count], *outs, *refs[count + skipped + results :])

    return pl.pallas_call(
        body,
        out_shape=out_shape,
        in_specs=specs,
        out_specs=result_specs,
        input_output_aliases=aliases,
        scratch_shapes=list(scratch),
        compiler_params=pltpu.CompilerParams(vmem_limit_bytes=vmem),
        cost_estimate=pl.CostEstimate(flops=int(cost * FLOPS_PER_US), bytes_accessed=0, transcendentals=0),
        name=name,
    )(*operands, *after, *passed)


def chunk_rows(ref):
    rounds, samples = ref.shape
    return jnp.concatenate(
        [ref[r : r + 1, k : k + LANES] for r in range(rounds) for k in range(0, samples, LANES)], axis=0
    )


FAR = 2.0**64


def pick_kernel(cap, slots, picks_hbm, points_hbm, assign_hbm, out_ref, points_ref, picks_ref, assign_ref, sems):
    picks_copy = pltpu.make_async_copy(picks_hbm, picks_ref, sems.at[0])
    assign_copy = pltpu.make_async_copy(assign_hbm, assign_ref, sems.at[1])
    points_copy = pltpu.make_async_copy(points_hbm, points_ref, sems.at[2])
    picks_copy.start()
    assign_copy.start()
    points_copy.start()
    picks_copy.wait()
    rounds = picks_ref.shape[0]
    per_round = picks_ref.shape[1] // LANES
    chunks = rounds * per_round
    point_count = points_ref.shape[0]
    local = chunk_rows(picks_ref) - device_index() * point_count
    owned = (local >= 0) & (local < point_count)
    flags = owned.astype(F32).astype(BF16)
    lower = (iota((LANES, LANES), 0) <= iota((LANES, LANES), 1)).astype(F32).astype(BF16)
    inside = jnp.dot(flags, lower, preferred_element_type=F32)
    sums = jnp.dot(flags, jnp.ones((LANES, LANES), BF16), preferred_element_type=F32)
    first, second = iota((chunks, chunks), 0), iota((chunks, chunks), 1)
    same = lax.div(first, per_round) == lax.div(second, per_round)
    earlier = (same & (second < first)).astype(F32).astype(BF16)
    before = jnp.dot(earlier, sums.astype(BF16), preferred_element_type=F32)
    round_of = lax.div(iota((chunks, LANES), 0), per_round)
    slot = (inside + before).astype(jnp.int32) - 1 + round_of * cap
    slot = jnp.where(owned, slot, -1)
    slot_ids = iota((slots, LANES), 0)
    found = jnp.zeros((slots, LANES), jnp.int32)
    for t in range(chunks):
        found = found + jnp.where(slot[t : t + 1, :] == slot_ids, local[t : t + 1, :] + 1, 0)
    place = jnp.sum(found.astype(F32), axis=1, keepdims=True).astype(jnp.int32)
    chosen = (iota((slots, point_count), 1) + 1 == place).astype(F32).astype(BF16)
    assign_copy.wait()
    ids = assign_ref[...]
    ids = jnp.concatenate([lax.div(ids, LANES), lax.rem(ids, LANES)], axis=1).astype(F32)
    points_copy.wait()
    rows = jnp.dot(chosen, points_ref[...], preferred_element_type=F32)
    rows = jnp.where(place > 0, rows, FAR)
    out_ref[...] = jnp.concatenate([rows, ids], axis=0).astype(BF16)


def add_tally(count, ids):
    lane_rows = iota((LANES, LANES), 0).astype(F32)
    chunk_ids = iota(count.shape, 0).astype(F32)
    ids = ids.astype(F32)
    for start in range(0, ids.shape[0], 8):
        rows = [ids[t : t + 1, :] for t in range(start, start + 8)]
        high = [(row[:, :LANES] == chunk_ids).astype(F32) for row in rows]
        low = [(row[:, LANES:] == lane_rows).astype(F32) for row in rows]
        high = jnp.concatenate(high, axis=1).astype(BF16)
        low = jnp.concatenate(low, axis=1).astype(BF16)
        count = count + nt_dot(high, low)
    return count


def tally_kernel(first, count_ref, *refs):
    count = count_ref[...]
    for ref in refs[:-1]:
        count = add_tally(count, ref[first:, :])
    refs[-1][...] = count


def holders_in_order(doubling, device_ids):
    if not doubling:
        return device_ids
    me = device_index()
    core = lax.rem(lax.div(me, CORE), 2)
    other = lax.div(device_ids, 16)
    kind = core ^ other
    mask = other * CORE
    for bit, masks in enumerate((*zip(*FAN), *zip(*SPREAD))):
        present = lax.rem(lax.div(device_ids, 1 << bit), 2)
        mask = mask ^ (present * jnp.where(kind == 0, masks[0], masks[1]))
    return me ^ mask


def slot_kernel(doubling, cap, slots, device_count, point_count, picks_ref, owner_ref, place_ref, slot_owner_ref, token_ref):
    token_ref[...] = jnp.zeros(token_ref.shape, F32)
    picks = chunk_rows(picks_ref)
    chunks = picks.shape[0]
    rounds = picks_ref.shape[0]
    per_round = chunks // rounds
    cand_chunks = owner_ref.shape[0]
    slot_chunks = slot_owner_ref.shape[0]
    lane_rows = iota((LANES, LANES), 0)
    lower = (lane_rows <= iota((LANES, LANES), 1)).astype(F32).astype(BF16)
    ones = jnp.ones((LANES, LANES), BF16)
    device_ids = iota((device_count, LANES), 0)
    first_chunk = cand_chunks - chunks
    holders = holders_in_order(doubling, device_ids)
    owners = jnp.zeros((2 * slot_chunks, LANES), F32)
    for r in range(rounds):
        carry = jnp.zeros((device_count, LANES), F32)
        for u in range(per_round):
            t = r * per_round + u
            holder = lax.div(picks[t : t + 1, :], point_count)
            held = (holder == device_ids).astype(F32)
            running = jnp.dot(held.astype(BF16), lower, preferred_element_type=F32) + carry
            carry = carry + jnp.dot(held.astype(BF16), ones, preferred_element_type=F32)
            rank = jnp.sum(held * running, axis=0, keepdims=True).astype(jnp.int32) - 1
            block = jnp.sum(jnp.where(holders == holder, device_ids, 0), axis=0, keepdims=True)
            place = block * slots + r * cap + rank
            place_ref[t : t + 1, :] = place
            high = lax.div(place, LANES) == iota((slot_chunks, LANES), 0)
            low = (lax.rem(place, LANES) == lane_rows).astype(F32).astype(BF16)
            tag = owner_ref[first_chunk + t : first_chunk + t + 1, :] + 1
            coarse = jnp.where(high, lax.div(tag, 32).astype(F32), 0.0)
            fine = jnp.where(high, lax.rem(tag, 32).astype(F32), 0.0)
            owners = owners + nt_dot(jnp.concatenate([coarse, fine], axis=0).astype(BF16), low)
    slot_owner_ref[...] = (owners[:slot_chunks] * 32.0 + owners[slot_chunks:]).astype(jnp.int32) - 1


def scan_rows(points, piece, best):
    wide = piece.astype(F32)
    half = 0.5 * jnp.sum(wide * wide, axis=1, keepdims=True)
    score = nt_dot(piece, points) - half
    for k in range(0, piece.shape[0], 8):
        best = jnp.maximum(best, score[k : k + 8, :])
    return best


def scan_table(points_ref, table_ref, first, rows, best):
    points = points_ref[...]
    step = min(256, rows)
    if rows <= 4096:
        for start in range(first, first + rows, step):
            best = scan_rows(points, table_ref[start : start + step, :], best)
        return best

    def visit(i, best):
        return scan_rows(points, table_ref[pl.ds(pl.multiple_of(i * step, step), step), :], best)

    return lax.fori_loop(0, rows // step, visit, best)


def first_scan_kernel(points_ref, centres_ref, best_ref, norm_ref):
    best_ref[...] = scan_table(points_ref, centres_ref, 0, centres_ref.shape[0], jnp.full(best_ref.shape, -jnp.inf, F32))
    wide = points_ref[...].astype(F32)
    square = wide * wide
    top = square.astype(BF16)
    rest = (square - top.astype(F32)).astype(BF16)
    ones = jnp.ones((8, square.shape[1]), BF16)
    norm_ref[...] = nt_dot(ones, top) + nt_dot(ones, rest)


def scan_pieces(points_ref, piece_refs, rows, best):
    for piece_ref in piece_refs:
        best = scan_table(points_ref, piece_ref, 0, rows, best)
    return best


def own_scan_kernel(slot_args, rows, points_ref, beside_ref, centres_ref, picks_ref, owner_ref, piece_ref, *refs):
    best_ref, beside_best_ref, norm_ref, place_ref, slot_owner_ref, token_ref = refs
    first_scan_kernel(points_ref, centres_ref, best_ref, norm_ref)
    best_ref[...] = scan_pieces(points_ref, [piece_ref], rows, best_ref[...])
    lowest = jnp.full(best_ref.shape, -jnp.inf, F32)
    beside_best_ref[...] = scan_pieces(beside_ref, [piece_ref], rows, lowest)
    slot_kernel(*slot_args, picks_ref, owner_ref, place_ref, slot_owner_ref, token_ref)


def both_scan_kernel(rows, points_ref, beside_ref, best_ref, beside_best_ref, piece_ref, *refs):
    next_ref, next_beside_ref, count_ref = refs
    next_ref[...] = scan_pieces(points_ref, [piece_ref], rows, best_ref[...])
    next_beside_ref[...] = scan_pieces(beside_ref, [piece_ref], rows, beside_best_ref[...])
    count_ref[...] = add_tally(jnp.zeros(count_ref.shape, F32), piece_ref[rows:, :])


def beside_scan_kernel(rows, beside_ref, best_ref, *refs):
    top_ref, token_ref = refs[-2:]
    token_ref[...] = jnp.zeros(token_ref.shape, F32)
    top_ref[...] = jnp.max(scan_pieces(beside_ref, refs[:-2], rows, best_ref[...]), axis=0, keepdims=True)


def next_scan_kernel(rows, points_ref, best_ref, start_ref, *refs):
    refs[-1][...] = jnp.max(scan_pieces(points_ref, refs[:-1], rows, best_ref[...]), axis=0, keepdims=True)


def near_kernel(norm_ref, top_ref, beside_ref, near_ref, share_ref):
    top = jnp.maximum(top_ref[...], beside_ref[...])
    near = jnp.maximum(norm_ref[0:1, :] - 2.0 * top, 0.0)
    near_ref[...] = near
    share_ref[...] = jnp.broadcast_to(jnp.sum(near, axis=1, keepdims=True)[None], share_ref.shape)


def lloyd_kernel(piece_rows, sides, count_refs, owner_ref, place_ref, slot_owner_ref, centres_ref, *refs):
    piece_refs, out_refs = refs[:-sides], refs[-sides:]
    finals, features = out_refs[0].shape[0], centres_ref.shape[1]
    slot_chunks = slot_owner_ref.shape[0]
    chunks = place_ref.shape[0]
    first_chunks = owner_ref.shape[0] - chunks
    count = sum(ref[...] for ref in count_refs)
    weights = 1.0 + count
    weight_top = weights.astype(BF16).astype(F32)
    weight_rest = (weights - weight_top).astype(BF16).astype(F32)
    lane_rows = iota((LANES, LANES), 0)
    placed = jnp.zeros((2 * slot_chunks, LANES), F32)
    for t in range(chunks):
        place = place_ref[t : t + 1, :]
        high = lax.div(place, LANES) == iota((slot_chunks, LANES), 0)
        low = (lax.rem(place, LANES) == lane_rows).astype(F32).astype(BF16)
        c = first_chunks + t
        both = [jnp.where(high, w[c : c + 1, :], 0.0) for w in (weight_top, weight_rest)]
        placed = placed + nt_dot(jnp.concatenate(both, axis=0).astype(BF16), low)
    row = lax.axis_index("row")
    side = lax.rem(row, sides)
    place = iota((sides * finals, LANES), 0)
    targets = place + row * finals
    if sides == 2:
        targets = jnp.where(place < finals, targets, targets - finals + (1 - 2 * side) * finals)

    def members(owners, tops, rests, mass):
        parts = []
        for b in range(owners.shape[0]):
            mine = owners[b : b + 1, :] == targets
            top = jnp.where(mine, tops[b : b + 1, :], 0.0)
            rest = jnp.where(mine, rests[b : b + 1, :], 0.0)
            mass = mass + (top + rest)
            parts.append(jnp.concatenate([top, rest], axis=0).astype(BF16))
        return jnp.concatenate(parts, axis=1), mass

    def share(values):
        height = first_chunks // sides
        return values[:height] if sides == 1 else jnp.where(side == 0, values[:height], values[height : 2 * height])

    mass = jnp.zeros((sides * finals, LANES), F32)
    member, mass = members(share(owner_ref[...]), share(weight_top), share(weight_rest), mass)
    height = centres_ref.shape[0] // sides
    table = centres_ref[pl.ds(pl.multiple_of(side * height, height), height), :]
    total = jnp.dot(member, table, preferred_element_type=F32)
    start = 0
    for piece_ref in piece_refs:
        stop = start + piece_rows // LANES
        member, mass = members(
            slot_owner_ref[start:stop, :], placed[start:stop], placed[slot_chunks + start : slot_chunks + stop], mass
        )
        total = total + jnp.dot(member, piece_ref[:piece_rows, :], preferred_element_type=F32)
        start = stop
    total = total[: sides * finals] + total[sides * finals :]
    for k, out_ref in enumerate(out_refs):
        out_ref[:, :features] = total[k * finals : (k + 1) * finals]
        out_ref[:, features:] = mass[k * finals : (k + 1) * finals]


def centre_kernel(*refs):
    part_refs, (out_ref, token_ref) = refs[:-2], refs[-2:]
    token_ref[...] = jnp.zeros(token_ref.shape, F32)
    features = out_ref.shape[1]
    total = sum(ref[:, :features] for ref in part_refs)
    out_ref[...] = total / jnp.sum(sum(ref[:, features:] for ref in part_refs), axis=1, keepdims=True)


def finish_kernel(total_points, near_ref, share_ref, token_ref, relative_ref):
    cost = jnp.sum(share_ref[...], axis=0)[0:1, 0:1]
    relative_ref[...] = near_ref[...] * total_points / cost


def permute(value, masks):
    pairs = [(d, d ^ masks[(d // CORE) % 2]) for d in range(lax.axis_size(AXES))]
    return lax.ppermute(value, AXES, pairs)


def hop(index):
    masks = tuple(zip(*FAN)) + tuple(zip(*SPREAD))
    return masks[index]


def done_after(value, *tokens):
    ready = tokens[0] >= 0.0
    for token in tokens[1:]:
        ready = ready & (token >= 0.0)
    return jnp.where(ready[:, : value.shape[1]], value, jnp.zeros_like(value))


def both_hops(first, second):
    return tuple(a ^ b for a, b in zip(first, second))


def shards(points, centres, picks, assign_pts, cand_assign):
    point_count, feature_count = points.shape
    row_count, col_count = lax.axis_size("row"), lax.axis_size("col")
    device_count = row_count * col_count
    doubling = (row_count, col_count) == (8, 4)
    round_count, sample_count = picks.shape
    cand_count = centres.shape[0] + round_count * sample_count
    cap = min(point_count, sample_count, -(-2 * sample_count // device_count))
    slots = -(-round_count * cap // 16) * 16
    slot_chunks = device_count * slots // LANES
    chunks = round_count * sample_count // LANES
    finals = K_FINAL // row_count
    shape = jax.ShapeDtypeStruct

    token = shape((1, feature_count), F32)
    count_shape = shape((cand_count // LANES, LANES), F32)
    id_rows = point_count // LANES
    piece_rows = slots * (4 if doubling else device_count)
    block, near_points = local_call(
        functools.partial(pick_kernel, cap, slots),
        (shape((slots + id_rows, feature_count), BF16), shape(points.shape, BF16)),
        (picks, points, assign_pts.reshape(id_rows, LANES)),
        "pick_rows",
        0.8,
        unread=(0, 1, 2),
        scratch=(
            pltpu.VMEM(picks.shape, jnp.int32),
            pltpu.VMEM((id_rows, LANES), jnp.int32),
            pltpu.SemaphoreType.DMA((3,)),
        ),
    )
    owner_rows = cand_assign.reshape(-1, LANES)
    best_shape = shape((8, point_count), F32)
    top_shape = shape((1, point_count), F32)
    held_chunks = slot_chunks // 2 if doubling else slot_chunks
    slot_shapes = (shape((chunks, LANES), jnp.int32), shape((held_chunks, LANES), jnp.int32))
    slot_args = (doubling, cap, slots, device_count, point_count)
    def next_scan(points, best, start, *pieces):
        cost = 0.2 + 0.8e-3 * piece_rows * len(pieces)
        kernel = functools.partial(next_scan_kernel, piece_rows)
        return local_call(kernel, top_shape, (points, best, start, *pieces), "scan_next", cost)

    near_shapes = (top_shape, shape((device_count, 1, LANES), F32))
    sum_shape = shape((finals, feature_count + LANES), F32)

    def centres_of(parts):
        return local_call(
            centre_kernel, (shape((finals, feature_count), F32), token), parts, "new_centres", 0.5
        )

    if doubling:
        swap = (CORE, CORE)
        near = [block, *(permute(block, m) for m in (hop(0), hop(1), both_hops(hop(0), hop(1))))]
        own = [part[:slots] for part in near] + [part[slots:] for part in near]
        own = jnp.concatenate(own, axis=0)
        others = [permute(own, m) for m in (hop(2), hop(3), both_hops(hop(2), hop(3)))]
        beside = permute(near_points, swap)
        best, beside_best, norms, places, slot_owners, scanned = local_call(
            functools.partial(own_scan_kernel, slot_args, piece_rows),
            (best_shape, best_shape, best_shape, *slot_shapes, token),
            (near_points, beside, centres, picks, owner_rows, own),
            "scan_own",
            3.0,
        )
        best, beside_best, counts = local_call(
            functools.partial(both_scan_kernel, piece_rows),
            (best_shape, best_shape, count_shape),
            (near_points, beside, best, beside_best, others[0]),
            "scan_both",
            1.3,
        )
        message, scanned = local_call(
            functools.partial(beside_scan_kernel, piece_rows),
            (top_shape, token),
            (beside, beside_best, *others[1:]),
            "scan_beside",
            0.9,
        )
        answer = permute(message, swap)
        top = next_scan(near_points, best, scanned, *others[1:])
        near, share = local_call(near_kernel, near_shapes, (norms, top, answer), "nearest", 0.5)
        shares = lax.all_to_all(share, AXES, 0, 0)

        def both_sides(mine_ref, other_ref, *refs):
            lloyd_kernel(piece_rows, 2, (mine_ref, other_ref), *refs)

        def rest_of_tally(near_ref, *refs):
            tally_kernel(piece_rows, *refs)

        def sum_up(near, counts, *operands):
            own, *others = operands[-4:]
            counts = local_call(rest_of_tally, count_shape, (near, counts, own, *others[1:]), "tally", 1.2)
            operands = (counts, permute(counts, swap), *operands)
            keep, give = local_call(both_sides, (sum_shape, sum_shape), operands, "lloyd", 1.8)
            return centres_of((keep, permute(give, swap)))

        def nothing(*operands):
            return jnp.zeros((finals, feature_count), F32), jnp.zeros(token.shape, F32)

        operands = (near, counts, owner_rows, places, slot_owners, centres, own, *others)
        new_centres, summed = lax.cond(lax.axis_index("row") < K_FINAL, sum_up, nothing, *operands)
    else:
        best, norms = local_call(
            first_scan_kernel, (best_shape, best_shape), (near_points, centres), "scan_centres", 1.6
        )
        places, slot_owners, found = local_call(
            functools.partial(slot_kernel, *slot_args), (*slot_shapes, token), (picks, owner_rows), "slot_owners", 1.0
        )
        counts = jnp.zeros(count_shape.shape, F32)
        counts = local_call(functools.partial(tally_kernel, 0), count_shape, (counts, block[slots:]), "tally", 0.3)
        counts = lax.psum(counts, AXES)
        table = lax.all_gather(block[:slots], AXES, tiled=True)
        top = next_scan(near_points, best, found, table)

        near, share = local_call(near_kernel, near_shapes, (norms, top, top), "nearest", 0.5)
        shares = lax.psum(share[:1], AXES)

        def one_side(count_ref, *refs):
            lloyd_kernel(piece_rows, 1, (count_ref,), *refs)

        operands = (counts, owner_rows, places, slot_owners, centres, table)
        new_centres, summed = centres_of((local_call(one_side, sum_shape, operands, "lloyd", 1.8),))
    relative = local_call(
        functools.partial(finish_kernel, float(point_count * device_count)),
        shape((1, point_count), F32),
        (near, shares, summed),
        "finish",
        0.6,
    )
    return (relative.reshape(-1), new_centres)


def solution(mesh):
    placed = (P(AXES, None), P(), P(), P(AXES), P())
    return jax.shard_map(
        shards,
        mesh=mesh,
        in_specs=placed,
        out_specs=(P(AXES), P("row", None)),
        check_vma=False,
    )
```

```python
import functools

import jax
import jax.numpy as jnp
from jax import lax
from jax.experimental import pallas as pl
from jax.experimental.pallas import tpu as pltpu
from jax.sharding import PartitionSpec as P

K_FINAL = 1024
AXES = ("row", "col")
LANES = 128
VMEM_LIMIT = 20 * 1024 * 1024
FLOPS_PER_US = 1.0e9
F32 = jnp.float32
BF16 = jnp.bfloat16

CORE = 4
FAN = ((3, 2), (24, 16))
SPREAD = ((24, 16), (2, 3))


def nt_dot(left, right):
    return lax.dot_general(left, right, (((1,), (1,)), ((), ())), preferred_element_type=F32)


def iota(shape, axis):
    return lax.broadcasted_iota(jnp.int32, shape, axis)


def device_index():
    return lax.axis_index("row") * lax.axis_size("col") + lax.axis_index("col")


def whole_spec():
    return pl.BlockSpec(memory_space=pltpu.VMEM)


def local_call(kernel, out_shape, operands, name, cost, after=(), unread=(), scratch=(), passed=(), vmem=VMEM_LIMIT):
    untouched = pl.BlockSpec(memory_space=pl.ANY)
    specs = [whole_spec()] * len(operands) + [untouched] * (len(after) + len(passed))
    result_specs = jax.tree.map(lambda _: whole_spec(), out_shape)
    aliases = {}
    if passed:
        first = len(operands) + len(after)
        aliases = {first + i: len(out_shape) + i for i in range(len(passed))}
        out_shape = (*out_shape, *(jax.ShapeDtypeStruct(x.shape, x.dtype) for x in passed))
        result_specs = (*result_specs, *[untouched] * len(passed))
    operands = list(operands)
    for place in unread:
        specs[place] = pl.BlockSpec(memory_space=pltpu.HBM)
        operands[place] = pltpu.with_memory_space_constraint(operands[place], pltpu.HBM)
    count = len(operands)

    skipped = len(after) + len(passed)
    results = len(out_shape) if isinstance(out_shape, tuple) else 1

    def body(*refs):
        outs = refs[count + skipped : count + skipped + results - len(passed)]
        kernel(*refs[:count], *outs, *refs[count + skipped + results :])

    return pl.pallas_call(
        body,
        out_shape=out_shape,
        in_specs=specs,
        out_specs=result_specs,
        input_output_aliases=aliases,
        scratch_shapes=list(scratch),
        compiler_params=pltpu.CompilerParams(vmem_limit_bytes=vmem),
        cost_estimate=pl.CostEstimate(flops=int(cost * FLOPS_PER_US), bytes_accessed=0, transcendentals=0),
        name=name,
    )(*operands, *after, *passed)


def chunk_rows(ref):
    rounds, samples = ref.shape
    return jnp.concatenate(
        [ref[r : r + 1, k : k + LANES] for r in range(rounds) for k in range(0, samples, LANES)], axis=0
    )


FAR = 2.0**64


def pick_kernel(cap, slots, picks_hbm, points_hbm, assign_hbm, out_ref, points_ref, picks_ref, assign_ref, sems):
    picks_copy = pltpu.make_async_copy(picks_hbm, picks_ref, sems.at[0])
    assign_copy = pltpu.make_async_copy(assign_hbm, assign_ref, sems.at[1])
    points_copy = pltpu.make_async_copy(points_hbm, points_ref, sems.at[2])
    picks_copy.start()
    assign_copy.start()
    points_copy.start()
    picks_copy.wait()
    rounds = picks_ref.shape[0]
    per_round = picks_ref.shape[1] // LANES
    chunks = rounds * per_round
    point_count = points_ref.shape[0]
    local = chunk_rows(picks_ref) - device_index() * point_count
    owned = (local >= 0) & (local < point_count)
    flags = owned.astype(F32).astype(BF16)
    lower = (iota((LANES, LANES), 0) <= iota((LANES, LANES), 1)).astype(F32).astype(BF16)
    inside = jnp.dot(flags, lower, preferred_element_type=F32)
    sums = jnp.dot(flags, jnp.ones((LANES, LANES), BF16), preferred_element_type=F32)
    first, second = iota((chunks, chunks), 0), iota((chunks, chunks), 1)
    same = lax.div(first, per_round) == lax.div(second, per_round)
    earlier = (same & (second < first)).astype(F32).astype(BF16)
    before = jnp.dot(earlier, sums.astype(BF16), preferred_element_type=F32)
    round_of = lax.div(iota((chunks, LANES), 0), per_round)
    slot = (inside + before).astype(jnp.int32) - 1 + round_of * cap
    slot = jnp.where(owned, slot, -1)
    slot_ids = iota((slots, LANES), 0)
    found = jnp.zeros((slots, LANES), jnp.int32)
    for t in range(chunks):
        found = found + jnp.where(slot[t : t + 1, :] == slot_ids, local[t : t + 1, :] + 1, 0)
    place = jnp.sum(found.astype(F32), axis=1, keepdims=True).astype(jnp.int32)
    chosen = (iota((slots, point_count), 1) + 1 == place).astype(F32).astype(BF16)
    assign_copy.wait()
    ids = assign_ref[...]
    ids = jnp.concatenate([lax.div(ids, LANES), lax.rem(ids, LANES)], axis=1).astype(F32)
    points_copy.wait()
    rows = jnp.dot(chosen, points_ref[...], preferred_element_type=F32)
    rows = jnp.where(place > 0, rows, FAR)
    out_ref[...] = jnp.concatenate([rows, ids], axis=0).astype(BF16)


def add_tally(count, ids):
    lane_rows = iota((LANES, LANES), 0).astype(F32)
    chunk_ids = iota(count.shape, 0).astype(F32)
    ids = ids.astype(F32)
    for start in range(0, ids.shape[0], 8):
        rows = [ids[t : t + 1, :] for t in range(start, start + 8)]
        high = [(row[:, :LANES] == chunk_ids).astype(F32) for row in rows]
        low = [(row[:, LANES:] == lane_rows).astype(F32) for row in rows]
        high = jnp.concatenate(high, axis=1).astype(BF16)
        low = jnp.concatenate(low, axis=1).astype(BF16)
        count = count + nt_dot(high, low)
    return count


def tally_kernel(first, count_ref, *refs):
    count = count_ref[...]
    for ref in refs[:-1]:
        count = add_tally(count, ref[first:, :])
    refs[-1][...] = count


def holders_in_order(doubling, device_ids):
    if not doubling:
        return device_ids
    me = device_index()
    core = lax.rem(lax.div(me, CORE), 2)
    other = lax.div(device_ids, 16)
    kind = core ^ other
    mask = other * CORE
    for bit, masks in enumerate((*zip(*FAN), *zip(*SPREAD))):
        present = lax.rem(lax.div(device_ids, 1 << bit), 2)
        mask = mask ^ (present * jnp.where(kind == 0, masks[0], masks[1]))
    return me ^ mask


def slot_kernel(doubling, cap, slots, device_count, point_count, picks_ref, owner_ref, place_ref, slot_owner_ref, token_ref):
    token_ref[...] = jnp.zeros(token_ref.shape, F32)
    picks = chunk_rows(picks_ref)
    chunks = picks.shape[0]
    rounds = picks_ref.shape[0]
    per_round = chunks // rounds
    cand_chunks = owner_ref.shape[0]
    slot_chunks = slot_owner_ref.shape[0]
    lane_rows = iota((LANES, LANES), 0)
    lower = (lane_rows <= iota((LANES, LANES), 1)).astype(F32).astype(BF16)
    ones = jnp.ones((LANES, LANES), BF16)
    device_ids = iota((device_count, LANES), 0)
    first_chunk = cand_chunks - chunks
    holders = holders_in_order(doubling, device_ids)
    owners = jnp.zeros((2 * slot_chunks, LANES), F32)
    for r in range(rounds):
        carry = jnp.zeros((device_count, LANES), F32)
        for u in range(per_round):
            t = r * per_round + u
            holder = lax.div(picks[t : t + 1, :], point_count)
            held = (holder == device_ids).astype(F32)
            running = jnp.dot(held.astype(BF16), lower, preferred_element_type=F32) + carry
            carry = carry + jnp.dot(held.astype(BF16), ones, preferred_element_type=F32)
            rank = jnp.sum(held * running, axis=0, keepdims=True).astype(jnp.int32) - 1
            block = jnp.sum(jnp.where(holders == holder, device_ids, 0), axis=0, keepdims=True)
            place = block * slots + r * cap + rank
            place_ref[t : t + 1, :] = place
            high = lax.div(place, LANES) == iota((slot_chunks, LANES), 0)
            low = (lax.rem(place, LANES) == lane_rows).astype(F32).astype(BF16)
            tag = owner_ref[first_chunk + t : first_chunk + t + 1, :] + 1
            coarse = jnp.where(high, lax.div(tag, 32).astype(F32), 0.0)
            fine = jnp.where(high, lax.rem(tag, 32).astype(F32), 0.0)
            owners = owners + nt_dot(jnp.concatenate([coarse, fine], axis=0).astype(BF16), low)
    slot_owner_ref[...] = (owners[:slot_chunks] * 32.0 + owners[slot_chunks:]).astype(jnp.int32) - 1


def scan_rows(points, piece, best):
    wide = piece.astype(F32)
    half = 0.5 * jnp.sum(wide * wide, axis=1, keepdims=True)
    score = nt_dot(piece, points) - half
    for k in range(0, piece.shape[0], 8):
        best = jnp.maximum(best, score[k : k + 8, :])
    return best


def scan_table(points_ref, table_ref, first, rows, best):
    points = points_ref[...]
    step = min(256, rows)
    if rows <= 4096:
        for start in range(first, first + rows, step):
            best = scan_rows(points, table_ref[start : start + step, :], best)
        return best

    def visit(i, best):
        return scan_rows(points, table_ref[pl.ds(pl.multiple_of(i * step, step), step), :], best)

    return lax.fori_loop(0, rows // step, visit, best)


def first_scan_kernel(points_ref, centres_ref, best_ref, norm_ref):
    best_ref[...] = scan_table(points_ref, centres_ref, 0, centres_ref.shape[0], jnp.full(best_ref.shape, -jnp.inf, F32))
    wide = points_ref[...].astype(F32)
    square = wide * wide
    top = square.astype(BF16)
    rest = (square - top.astype(F32)).astype(BF16)
    ones = jnp.ones((8, square.shape[1]), BF16)
    norm_ref[...] = nt_dot(ones, top) + nt_dot(ones, rest)


def scan_pieces(points_ref, piece_refs, rows, best):
    for piece_ref in piece_refs:
        best = scan_table(points_ref, piece_ref, 0, rows, best)
    return best


def own_scan_kernel(slot_args, rows, points_ref, centres_ref, picks_ref, owner_ref, piece_ref, *refs):
    best_ref, norm_ref, place_ref, slot_owner_ref, token_ref = refs
    first_scan_kernel(points_ref, centres_ref, best_ref, norm_ref)
    best_ref[...] = scan_pieces(points_ref, [piece_ref], rows, best_ref[...])
    slot_kernel(*slot_args, picks_ref, owner_ref, place_ref, slot_owner_ref, token_ref)


def both_scan_kernel(rows, points_ref, beside_ref, best_ref, own_ref, piece_ref, *refs):
    next_ref, next_count_ref, beside_best_ref = refs
    next_ref[...] = scan_pieces(points_ref, [piece_ref], rows, best_ref[...])
    next_count_ref[...] = add_tally(jnp.zeros(next_count_ref.shape, F32), piece_ref[rows:, :])
    lowest = jnp.full(beside_best_ref.shape, -jnp.inf, F32)
    beside_best_ref[...] = scan_pieces(beside_ref, [own_ref, piece_ref], rows, lowest)


def beside_scan_kernel(rows, beside_ref, best_ref, *refs):
    top_ref, token_ref = refs[-2:]
    token_ref[...] = jnp.zeros(token_ref.shape, F32)
    top_ref[...] = jnp.max(scan_pieces(beside_ref, refs[:-2], rows, best_ref[...]), axis=0, keepdims=True)


def next_scan_kernel(rows, points_ref, best_ref, start_ref, *refs):
    refs[-1][...] = jnp.max(scan_pieces(points_ref, refs[:-1], rows, best_ref[...]), axis=0, keepdims=True)


def near_kernel(norm_ref, top_ref, beside_ref, near_ref, share_ref):
    top = jnp.maximum(top_ref[...], beside_ref[...])
    near = jnp.maximum(norm_ref[0:1, :] - 2.0 * top, 0.0)
    near_ref[...] = near
    share_ref[...] = jnp.broadcast_to(jnp.sum(near, axis=1, keepdims=True), share_ref.shape)


def lloyd_kernel(piece_rows, sides, count_refs, owner_ref, place_ref, slot_owner_ref, centres_ref, *refs):
    piece_refs, out_refs = refs[:-sides], refs[-sides:]
    finals, features = out_refs[0].shape[0], centres_ref.shape[1]
    slot_chunks = slot_owner_ref.shape[0]
    chunks = place_ref.shape[0]
    first_chunks = owner_ref.shape[0] - chunks
    count = sum(ref[...] for ref in count_refs)
    weights = 1.0 + count
    weight_top = weights.astype(BF16).astype(F32)
    weight_rest = (weights - weight_top).astype(BF16).astype(F32)
    lane_rows = iota((LANES, LANES), 0)
    placed = jnp.zeros((2 * slot_chunks, LANES), F32)
    for t in range(chunks):
        place = place_ref[t : t + 1, :]
        high = lax.div(place, LANES) == iota((slot_chunks, LANES), 0)
        low = (lax.rem(place, LANES) == lane_rows).astype(F32).astype(BF16)
        c = first_chunks + t
        both = [jnp.where(high, w[c : c + 1, :], 0.0) for w in (weight_top, weight_rest)]
        placed = placed + nt_dot(jnp.concatenate(both, axis=0).astype(BF16), low)
    row = lax.axis_index("row")
    side = lax.rem(row, sides)
    place = iota((sides * finals, LANES), 0)
    targets = place + row * finals
    if sides == 2:
        targets = jnp.where(place < finals, targets, targets - finals + (1 - 2 * side) * finals)

    def members(owners, tops, rests, mass):
        parts = []
        for b in range(owners.shape[0]):
            mine = owners[b : b + 1, :] == targets
            top = jnp.where(mine, tops[b : b + 1, :], 0.0)
            rest = jnp.where(mine, rests[b : b + 1, :], 0.0)
            mass = mass + (top + rest)
            parts.append(jnp.concatenate([top, rest], axis=0).astype(BF16))
        return jnp.concatenate(parts, axis=1), mass

    def share(values):
        height = first_chunks // sides
        return values[:height] if sides == 1 else jnp.where(side == 0, values[:height], values[height : 2 * height])

    mass = jnp.zeros((sides * finals, LANES), F32)
    member, mass = members(share(owner_ref[...]), share(weight_top), share(weight_rest), mass)
    height = centres_ref.shape[0] // sides
    table = centres_ref[pl.ds(pl.multiple_of(side * height, height), height), :]
    total = jnp.dot(member, table, preferred_element_type=F32)
    start = 0
    for piece_ref in piece_refs:
        stop = start + piece_rows // LANES
        member, mass = members(
            slot_owner_ref[start:stop, :], placed[start:stop], placed[slot_chunks + start : slot_chunks + stop], mass
        )
        total = total + jnp.dot(member, piece_ref[:piece_rows, :], preferred_element_type=F32)
        start = stop
    total = total[: sides * finals] + total[sides * finals :]
    for k, out_ref in enumerate(out_refs):
        out_ref[:, :features] = total[k * finals : (k + 1) * finals]
        out_ref[:, features:] = mass[k * finals : (k + 1) * finals]


def centre_kernel(*refs):
    part_refs, (out_ref, token_ref) = refs[:-2], refs[-2:]
    token_ref[...] = jnp.zeros(token_ref.shape, F32)
    features = out_ref.shape[1]
    total = sum(ref[:, :features] for ref in part_refs)
    out_ref[...] = total / jnp.sum(sum(ref[:, features:] for ref in part_refs), axis=1, keepdims=True)


def finish_kernel(total_points, near_ref, share_ref, token_ref, relative_ref):
    cost = jnp.sum(share_ref[...], axis=0, keepdims=True)[:, 0:1]
    relative_ref[...] = near_ref[...] * total_points / cost


def permute(value, masks):
    pairs = [(d, d ^ masks[(d // CORE) % 2]) for d in range(lax.axis_size(AXES))]
    return lax.ppermute(value, AXES, pairs)


def hop(index):
    masks = tuple(zip(*FAN)) + tuple(zip(*SPREAD))
    return masks[index]


def done_after(value, *tokens):
    ready = tokens[0] >= 0.0
    for token in tokens[1:]:
        ready = ready & (token >= 0.0)
    return jnp.where(ready[:, : value.shape[1]], value, jnp.zeros_like(value))


def both_hops(first, second):
    return tuple(a ^ b for a, b in zip(first, second))


def shards(points, centres, picks, assign_pts, cand_assign):
    point_count, feature_count = points.shape
    row_count, col_count = lax.axis_size("row"), lax.axis_size("col")
    device_count = row_count * col_count
    doubling = (row_count, col_count) == (8, 4)
    round_count, sample_count = picks.shape
    cand_count = centres.shape[0] + round_count * sample_count
    cap = min(point_count, sample_count, -(-2 * sample_count // device_count))
    slots = -(-round_count * cap // 16) * 16
    slot_chunks = device_count * slots // LANES
    chunks = round_count * sample_count // LANES
    finals = K_FINAL // row_count
    shape = jax.ShapeDtypeStruct

    token = shape((1, feature_count), F32)
    count_shape = shape((cand_count // LANES, LANES), F32)
    id_rows = point_count // LANES
    piece_rows = slots * (4 if doubling else device_count)
    block, near_points = local_call(
        functools.partial(pick_kernel, cap, slots),
        (shape((slots + id_rows, feature_count), BF16), shape(points.shape, BF16)),
        (picks, points, assign_pts.reshape(id_rows, LANES)),
        "pick_rows",
        0.8,
        unread=(0, 1, 2),
        scratch=(
            pltpu.VMEM(picks.shape, jnp.int32),
            pltpu.VMEM((id_rows, LANES), jnp.int32),
            pltpu.SemaphoreType.DMA((3,)),
        ),
    )
    owner_rows = cand_assign.reshape(-1, LANES)
    best_shape = shape((8, point_count), F32)
    top_shape = shape((1, point_count), F32)
    held_chunks = slot_chunks // 2 if doubling else slot_chunks
    slot_shapes = (shape((chunks, LANES), jnp.int32), shape((held_chunks, LANES), jnp.int32))
    slot_args = (doubling, cap, slots, device_count, point_count)
    def next_scan(points, best, start, *pieces):
        cost = 0.2 + 0.8e-3 * piece_rows * len(pieces)
        kernel = functools.partial(next_scan_kernel, piece_rows)
        return local_call(kernel, top_shape, (points, best, start, *pieces), "scan_next", cost)

    near_shapes = (top_shape, shape((device_count, LANES), F32))
    sum_shape = shape((finals, feature_count + LANES), F32)

    def centres_of(parts):
        return local_call(
            centre_kernel, (shape((finals, feature_count), F32), token), parts, "new_centres", 0.5
        )

    if doubling:
        swap = (CORE, CORE)
        near = [block, *(permute(block, m) for m in (hop(0), hop(1), both_hops(hop(0), hop(1))))]
        own = [part[:slots] for part in near] + [part[slots:] for part in near]
        own = jnp.concatenate(own, axis=0)
        others = [permute(own, m) for m in (hop(2), hop(3), both_hops(hop(2), hop(3)))]
        best, norms, places, slot_owners, scanned = local_call(
            functools.partial(own_scan_kernel, slot_args, piece_rows),
            (best_shape, best_shape, *slot_shapes, token),
            (near_points, centres, picks, owner_rows, own),
            "scan_own",
            3.0,
        )
        beside = permute(near_points, swap)
        best, counts, beside_best = local_call(
            functools.partial(both_scan_kernel, piece_rows),
            (best_shape, count_shape, best_shape),
            (near_points, beside, best, own, others[0]),
            "scan_both",
            1.3,
        )
        message, scanned = local_call(
            functools.partial(beside_scan_kernel, piece_rows),
            (top_shape, token),
            (beside, beside_best, *others[1:]),
            "scan_beside",
            0.9,
        )
        answer = permute(message, swap)
        top = next_scan(near_points, best, scanned, *others[1:])
        near, share = local_call(near_kernel, near_shapes, (norms, top, answer), "nearest", 0.5)
        shares = lax.all_to_all(share, AXES, 0, 0)

        def both_sides(mine_ref, other_ref, *refs):
            lloyd_kernel(piece_rows, 2, (mine_ref, other_ref), *refs)

        def rest_of_tally(near_ref, *refs):
            tally_kernel(piece_rows, *refs)

        def sum_up(near, counts, *operands):
            own, *others = operands[-4:]
            counts = local_call(rest_of_tally, count_shape, (near, counts, own, *others[1:]), "tally", 1.2)
            operands = (counts, permute(counts, swap), *operands)
            keep, give = local_call(both_sides, (sum_shape, sum_shape), operands, "lloyd", 1.8)
            return centres_of((keep, permute(give, swap)))

        def nothing(*operands):
            return jnp.zeros((finals, feature_count), F32), jnp.zeros(token.shape, F32)

        operands = (near, counts, owner_rows, places, slot_owners, centres, own, *others)
        new_centres, summed = lax.cond(lax.axis_index("row") < K_FINAL, sum_up, nothing, *operands)
    else:
        best, norms = local_call(
            first_scan_kernel, (best_shape, best_shape), (near_points, centres), "scan_centres", 1.6
        )
        places, slot_owners, found = local_call(
            functools.partial(slot_kernel, *slot_args), (*slot_shapes, token), (picks, owner_rows), "slot_owners", 1.0
        )
        counts = jnp.zeros(count_shape.shape, F32)
        counts = local_call(functools.partial(tally_kernel, 0), count_shape, (counts, block[slots:]), "tally", 0.3)
        counts = lax.psum(counts, AXES)
        table = lax.all_gather(block[:slots], AXES, tiled=True)
        top = next_scan(near_points, best, found, table)

        near, share = local_call(near_kernel, near_shapes, (norms, top, top), "nearest", 0.5)
        shares = lax.psum(share[:1], AXES)

        def one_side(count_ref, *refs):
            lloyd_kernel(piece_rows, 1, (count_ref,), *refs)

        operands = (counts, owner_rows, places, slot_owners, centres, table)
        new_centres, summed = centres_of((local_call(one_side, sum_shape, operands, "lloyd", 1.8),))
    relative = local_call(
        functools.partial(finish_kernel, float(point_count * device_count)),
        shape((1, point_count), F32),
        (near, shares, summed),
        "finish",
        0.6,
    )
    return (relative.reshape(-1), new_centres)


def solution(mesh):
    placed = (P(AXES, None), P(), P(), P(AXES), P())
    return jax.shard_map(
        shards,
        mesh=mesh,
        in_specs=placed,
        out_specs=(P(AXES), P("row", None)),
        check_vma=False,
    )
```
